128 devices in a mesh: mrow: 4 (over x), mcol: 4 (over y), sub: 8 (over z, core).
Axes of the slice: x: 4, y: 4, z: 4, core: 2. Of those that a mesh axis runs over, the one named last changes fastest.
Arguments:
- deflation: bfloat16 [64, 64, 256, 1024], P(None, 'sub', 'mcol', 'mrow'), may hold values from -0.13258252 to 0.13258252
- reaction: float32 [64, 256, 1024], P('sub', 'mcol', 'mrow'), may hold values from 0.005 to 0.16
- vector_counts: int32 [128], P(('mrow', 'mcol', 'sub')), may hold values from 32 to 64
Outputs:
- coarse_factor: float32 [8192, 8192], P(('mrow', 'mcol', 'sub'))
The draws below stay inside these ranges and needn't reach their ends.
All inputs are finite; a program needn't handle non-finite values.
Results may differ from the reference program's by a relative error of at most 0.0003.
Values may be sent and summed in bfloat16 or wider, within the bound.
A program may use at most 192 MiB of HBM per device.

```python
import math
import jax
import jax.numpy as jnp
import numpy as np
from jax import lax

K = 64
CX = 8
CY = 64
CZ = 256
PANEL = 256
PANELS = 2
NX = 64
NY = 256
NZ = 1024
ORDER = 8192
N_MROW = 4
N_MCOL = 4
N_SUB = 8
DEVICES = 128


def wave_table(wave_key, rows_count, length):
    freq_key, angle_key = jax.random.split(wave_key)
    frequency = jax.random.uniform(freq_key, (rows_count, 1), jnp.float32, 0.02, 0.12)
    offset_angle = jax.random.uniform(angle_key, (rows_count, 1), jnp.float32, -math.pi, math.pi)
    return jnp.cos(frequency * jnp.arange(length).astype(jnp.float32)[None, :] + offset_angle)


def face_profile(length, cell_count):
    local_cell = (jnp.arange(length) % cell_count).astype(jnp.float32)
    return jnp.exp(-local_cell / 3.0) + jnp.exp(-(cell_count - 1 - local_cell) / 3.0)


def smooth_field(smooth_key):
    summed = jnp.zeros((K, NX, NY, NZ), jnp.float32)
    for term_index in range(2):
        term_key = jax.random.fold_in(smooth_key, term_index)
        magnitude = jax.random.uniform(jax.random.fold_in(term_key, 1), (K,), jnp.float32, 0.5, 1.0)
        sign_value = jnp.where(jax.random.bernoulli(jax.random.fold_in(term_key, 2), 0.5, (K,)), 1.0, -1.0)
        wave_x = wave_table(jax.random.fold_in(term_key, 3), K, NX)
        wave_y = wave_table(jax.random.fold_in(term_key, 4), K, NY)
        wave_z = wave_table(jax.random.fold_in(term_key, 5), K, NZ)
        weight_term = (magnitude * sign_value)[:, None, None, None]
        summed = summed + weight_term * wave_x[:, :, None, None] * wave_y[:, None, :, None] * wave_z[:, None, None, :]
    return summed


def draw_deflation(key, part):
    key = jax.random.fold_in(key, 7)
    grid_shape = (NX, NY, NZ)
    cell_counts = (CX, CY, CZ)
    face_cells = (CY * CZ, CX * CZ, CX * CY)
    main_axis = jax.random.randint(jax.random.fold_in(key, 1), (K,), 0, 3)
    strength = jax.random.uniform(jax.random.fold_in(key, 2), (K,), jnp.float32, 0.5, 1.5)
    summed = jnp.zeros((K, NX, NY, NZ), jnp.float32)
    for axis_number in range(3):
        axis_key = jax.random.fold_in(key, 10 + axis_number)
        amplitude = strength * jnp.where(main_axis == axis_number, 1.0, 0.35) / math.sqrt(face_cells[axis_number])
        rough_shape = [K, NX, NY, NZ]
        rough_shape[axis_number + 1] = 1
        rough_key = jax.random.fold_in(axis_key, 1)
        first_draw = jax.random.uniform(jax.random.fold_in(rough_key, 1), tuple(rough_shape), jnp.float32, 0.0, 1.0)
        second_draw = jax.random.uniform(jax.random.fold_in(rough_key, 2), tuple(rough_shape), jnp.float32, 0.0, 1.0)
        rough_factor = 1.0 + (first_draw + second_draw - 1.0) / 3.0
        profile_shape = [1, 1, 1, 1]
        profile_shape[axis_number + 1] = grid_shape[axis_number]
        profile = face_profile(grid_shape[axis_number], cell_counts[axis_number]).reshape(tuple(profile_shape))
        smooth = smooth_field(jax.random.fold_in(axis_key, 2))
        summed = summed + amplitude[:, None, None, None] * profile * smooth * rough_factor
    combined = summed + 0.5 * jnp.roll(summed, 1, axis=0)
    limit_value = 2.98 / math.sqrt(CX * CY)
    return jnp.clip(combined, -limit_value, limit_value).astype(jnp.bfloat16)


def draw_reaction(key, part):
    key = jax.random.fold_in(key, 11)
    level_shape = (NX // CX, NY // CY, NZ // CZ)
    level_table = jnp.exp(jax.random.uniform(jax.random.fold_in(key, 1), level_shape, jnp.float32, math.log(0.01), math.log(0.08)))
    spread = jnp.repeat(jnp.repeat(jnp.repeat(level_table, CX, axis=0), CY, axis=1), CZ, axis=2)
    factor_key = jax.random.fold_in(key, 2)
    factor = jax.random.uniform(factor_key, (NX, NY, NZ), jnp.float32, 0.5, 1.5)
    return (spread * factor).astype(jnp.float32)


def set_ends(result, own_key, low, top_value):
    longest = result.shape.index(max(result.shape))
    spots = []
    for shift in (0, 1):
        where = [jax.random.randint(jax.random.fold_in(own_key, axis), (), 0, length) for axis, length in enumerate(result.shape)]
        where[longest] = (where[longest] + shift) % result.shape[longest]
        spots.append(tuple(where))
    return result.at[spots[0]].set(low).at[spots[1]].set(top_value)


def setup_inputs(seed: int = 0) -> dict:
    splits = jax.random.split(jax.random.key(seed), 4)
    return {
        "deflation": draw_deflation(jax.random.fold_in(splits[3], 71), 0),
        "reaction": draw_reaction(jax.random.fold_in(splits[3], 71), 0),
        "vector_counts": set_ends(jax.random.randint(splits[2], (DEVICES,), K // 2, K + 1), jax.random.fold_in(splits[2], 1), K // 2, K).astype(jnp.int32),
    }


def apply_local(block, weight):
    padded = jnp.pad(block, ((0, 0), (1, 1), (1, 1), (1, 1)))
    beside = padded[:, 2:, 1:-1, 1:-1].astype(jnp.float32) + padded[:, :-2, 1:-1, 1:-1].astype(jnp.float32)
    beside = beside + padded[:, 1:-1, 2:, 1:-1].astype(jnp.float32) + padded[:, 1:-1, :-2, 1:-1].astype(jnp.float32)
    beside = beside + padded[:, 1:-1, 1:-1, 2:].astype(jnp.float32) + padded[:, 1:-1, 1:-1, :-2].astype(jnp.float32)
    return ((6.0 + weight)[None] * block.astype(jnp.float32) - beside).astype(jnp.bfloat16)

def couple(own_face, other_face):
    return -jnp.dot(own_face.reshape(K, -1).astype(jnp.float32), other_face.reshape(K, -1).T.astype(jnp.float32), preferred_element_type=jnp.float32)

def live_vectors(count):
    return (jnp.arange(K).astype(jnp.int32) < count).astype(jnp.bfloat16)

def as_index(value):
    return jnp.asarray(value).astype(jnp.int32)

def subdomain(block_id, deflation, reaction, vector_counts):
    block_id = as_index(block_id)
    zero_index = as_index(0)
    row_pos = block_id // (N_MCOL * N_SUB)
    col_pos = block_id // N_SUB % N_MCOL
    sub_pos = block_id % N_SUB
    first_x = as_index(sub_pos * CX)
    first_y = as_index(col_pos * CY)
    first_z = as_index(row_pos * CZ)
    live_own = live_vectors(vector_counts[block_id])
    own_part = lax.dynamic_slice(deflation, (zero_index, first_x, first_y, first_z), (K, CX, CY, CZ)) * live_own[:, None, None, None]
    weight = lax.dynamic_slice(reaction, (first_x, first_y, first_z), (CX, CY, CZ))
    applied = apply_local(own_part, weight)
    gram_block = jnp.dot(own_part.reshape(K, -1).astype(jnp.float32), applied.reshape(K, -1).T.astype(jnp.float32), preferred_element_type=jnp.float32)
    diagonal_block = 0.5 * (gram_block + gram_block.T) + jnp.diag(1.0 - live_own.astype(jnp.float32))
    last_id = as_index(DEVICES - 1)
    next_x = lax.dynamic_slice(deflation, (zero_index, as_index(first_x + CX), first_y, first_z), (K, 1, CY, CZ))[:, 0]
    next_x = next_x * live_vectors(vector_counts[jnp.minimum(block_id + 1, last_id)])[:, None, None]
    next_y = lax.dynamic_slice(deflation, (zero_index, first_x, as_index(first_y + CY), first_z), (K, CX, 1, CZ))[:, :, 0]
    next_y = next_y * live_vectors(vector_counts[jnp.minimum(block_id + N_SUB, last_id)])[:, None, None]
    next_z = lax.dynamic_slice(deflation, (zero_index, first_x, first_y, as_index(first_z + CZ)), (K, CX, CY, 1))[:, :, :, 0]
    next_z = next_z * live_vectors(vector_counts[jnp.minimum(block_id + N_SUB * N_MCOL, last_id)])[:, None, None]
    plus_x = couple(own_part[:, -1], next_x)
    plus_y = couple(own_part[:, :, -1], next_y)
    plus_z = couple(own_part[:, :, :, -1], next_z)
    return (diagonal_block, jnp.stack([plus_x, plus_y, plus_z]))

def reference(deflation, reaction, vector_counts):
    diagonals, couplings = lax.map(lambda block_id: subdomain(block_id, deflation, reaction, vector_counts), jnp.arange(DEVICES).astype(jnp.int32))
    coarse = jnp.zeros((DEVICES, K, DEVICES, K), jnp.float32)
    all_blocks = np.arange(DEVICES)
    coarse = coarse.at[all_blocks, :, all_blocks, :].set(diagonals)
    neighbours = ((0, 1, all_blocks % N_SUB != N_SUB - 1), (1, N_SUB, all_blocks // N_SUB % N_MCOL != N_MCOL - 1), (2, N_SUB * N_MCOL, all_blocks // (N_SUB * N_MCOL) != N_MROW - 1))
    for axis_number, stride, usable in neighbours:
        source = all_blocks[usable]
        pairs = couplings[source, axis_number]
        coarse = coarse.at[source, :, source + stride, :].set(pairs)
        coarse = coarse.at[source + stride, :, source, :].set(jnp.transpose(pairs, (0, 2, 1)))
    schur = coarse.reshape(ORDER, ORDER)
    rows_all = jnp.arange(ORDER).astype(jnp.int32)
    factors = []
    for panel_id in range(PANELS):
        first_col = panel_id * PANEL
        columns = schur[:, first_col:first_col + PANEL]
        pivot_factor = jnp.linalg.cholesky(columns[first_col:first_col + PANEL])
        panel_rows = jax.scipy.linalg.solve_triangular(pivot_factor, columns.T, lower=True).T
        panel_rows = jnp.where((rows_all >= first_col)[:, None], panel_rows, 0.0)
        schur = schur - jnp.dot(panel_rows.astype(jnp.float32), panel_rows.T.astype(jnp.float32), precision=lax.Precision.HIGHEST, preferred_element_type=jnp.float32)
        factors.append(panel_rows)
    finished = PANELS * PANEL
    trailing = jnp.where((rows_all >= finished)[:, None], schur[:, finished:], 0.0)
    return jnp.concatenate(factors + [trailing], axis=1)
```

```python
import functools

import jax
import jax.numpy as jnp
from jax import lax
from jax.experimental import pallas as pl
from jax.experimental.pallas import tpu as pltpu
from jax.sharding import PartitionSpec as P

MESH = pl.DeviceIdType.MESH
F32 = jnp.float32
BF16 = jnp.bfloat16
HI = lax.Precision.HIGHEST
K = 64
CX = 8
CY = 64
CZ = 256
ROWS = K * 8
SUB = 8


def dot_nt(a, b, precision=None):
    return lax.dot_general(
        a, b, (((1,), (1,)), ((), ())), precision=precision, preferred_element_type=F32
    )


def dot_nn(a, b, precision=None):
    return lax.dot_general(
        a, b, (((1,), (0,)), ((), ())), precision=precision, preferred_element_type=F32
    )


def dot_tn(a, b, precision=None):
    return lax.dot_general(
        a, b, (((0,), (0,)), ((), ())), precision=precision, preferred_element_type=F32
    )


def iota(shape, axis):
    return lax.broadcasted_iota(jnp.int32, shape, axis)


def fold(product):
    same = (iota(product.shape, 0) & 7) == (iota(product.shape, 1) & 7)
    kept = jnp.where(same, product, 0.0).reshape(K, 8, ROWS).sum(axis=1)
    collect = ((iota((ROWS, K), 0) >> 3) == iota((ROWS, K), 1)).astype(F32)
    return dot_nn(kept, collect, HI)


def assemble_kernel(
    defl,
    react,
    count,
    own_out,
    gathered,
    mbuf,
    left,
    right,
    acc,
    weight,
    zrows,
    ylow,
    yhigh,
    yrecv,
    zhigh,
    zrecv,
    xrecv_low,
    xrecv_high,
    mask_own,
    mask_recv,
    part_send,
    part_recv,
    load_sem,
    mask_send_sem,
    mask_recv_sem,
    face_send_sem,
    face_recv_sem,
    part_send_sem,
    part_recv_sem,
    line_send_sem,
    cross_send_sem,
    line_recv_sem,
):
    mrow = lax.axis_index("mrow")
    mcol = lax.axis_index("mcol")
    sub = lax.axis_index("sub")
    mrows = lax.axis_size("mrow")
    mcols = lax.axis_size("mcol")
    s_next, s_prev = lax.rem(sub + 1, SUB), lax.rem(sub + SUB - 1, SUB)
    j_next, j_prev = lax.rem(mcol + 1, mcols), lax.rem(mcol + mcols - 1, mcols)
    i_next, i_prev = lax.rem(mrow + 1, mrows), lax.rem(mrow + mrows - 1, mrows)

    loads = [
        pltpu.make_async_copy(defl.at[:, x], mbuf.at[x], load_sem.at[x]) for x in range(CX)
    ]
    for load in loads:
        load.start()

    barrier = pltpu.get_barrier_semaphore()
    for step in range(1, SUB):
        pl.semaphore_signal(
            barrier,
            inc=1,
            device_id={"sub": lax.rem(sub + step, SUB)},
            device_id_type=MESH,
        )
    for axis, other in (
        ("mcol", j_next),
        ("mcol", j_prev),
        ("mrow", i_next),
        ("mrow", i_prev),
    ):
        pl.semaphore_signal(barrier, inc=1, device_id={axis: other}, device_id_type=MESH)
    pl.semaphore_wait(barrier, SUB - 1 + 4)

    def remote(src, dst, send, recv, target):
        return pltpu.make_async_remote_copy(
            src_ref=src,
            dst_ref=dst,
            send_sem=send,
            recv_sem=recv,
            device_id=target,
            device_id_type=MESH,
        )

    xface_up = remote(
        defl.at[:, CX - 1, 0 : CY // 2],
        xrecv_low,
        face_send_sem.at[0],
        face_recv_sem.at[0],
        {"sub": s_next},
    )
    xface_down = remote(
        defl.at[:, 0, CY // 2 : CY],
        xrecv_high,
        face_send_sem.at[1],
        face_recv_sem.at[1],
        {"sub": s_prev},
    )
    xface_up.start()
    xface_down.start()

    live = count[0]
    mask_own[...] = (iota((8, 128), 1) < live).astype(F32)
    masks = []
    for slot, target in enumerate(
        (
            {"sub": s_next},
            {"sub": s_prev},
            {"mcol": j_next},
            {"mcol": j_prev},
            {"mrow": i_next},
            {"mrow": i_prev},
        )
    ):
        masks.append(
            remote(
                mask_own,
                mask_recv.at[slot],
                mask_send_sem.at[slot],
                mask_recv_sem.at[slot],
                target,
            )
        )
        masks[-1].start()

    weight[...] = 3.0 + 0.5 * react[...]
    mbuf[CX] = jnp.zeros((K, CY, CZ), BF16)
    acc[...] = jnp.zeros_like(acc)
    part_send[...] = jnp.zeros_like(part_send)
    tail = iota((16, 8 * CZ), 0)
    spot = (tail & 7) * CZ + (tail >> 3) * (CZ - 1)
    left[ROWS : ROWS + 16, :] = (iota((16, 8 * CZ), 1) == spot).astype(F32).astype(BF16)

    def rows_of(value, block):
        return value[:, 8 * block : 8 * block + 8, :].reshape(16, CZ).astype(BF16)

    def plane(x, carry):
        def pair(step, inner):
            first = pl.multiple_of(2 * step, 2)
            place = pl.ds(pl.multiple_of(16 * step, 16), 16)
            here = mbuf[x, pl.ds(first, 2)].astype(F32)
            after_x = mbuf[x + 1, pl.ds(first, 2)].astype(F32)
            after_y = pltpu.roll(here, CY - 1, 1)
            after_y = jnp.where(iota(here.shape, 1) == CY - 1, 0.0, after_y)
            after_z = pltpu.roll(here, CZ - 1, 2)
            after_z = jnp.where(iota(here.shape, 2) == CZ - 1, 0.0, after_z)
            half = weight[x][None] * here - after_x - after_y - after_z
            for block in range(8):
                lanes = slice(block * CZ, (block + 1) * CZ)
                left[place, lanes] = rows_of(half, block)
                right[place, lanes] = rows_of(here, block)
            return inner

        lax.fori_loop(0, K // 2, pair, 0)
        product = dot_nt(left[...], right[...])
        acc[...] += product[:ROWS]
        zrows[x] = product[ROWS : ROWS + 16]
        pick_row = iota((K, ROWS), 0) * 8
        pick_low = (iota((K, ROWS), 1) == pick_row).astype(F32).astype(BF16)
        pick_high = (iota((K, ROWS), 1) == pick_row + 7).astype(F32).astype(BF16)
        ylow[x] = dot_nn(pick_low, right[:, 0:CZ]).astype(BF16)
        yhigh[x] = dot_nn(pick_high, right[:, 7 * CZ : 8 * CZ]).astype(BF16)
        return carry

    for load in loads:
        load.wait()
    lax.fori_loop(0, CX, plane, 0)

    zhigh[...] = zrows[:, 8:16, :].reshape(K, ROWS).astype(BF16)
    yface = remote(yhigh, yrecv, face_send_sem.at[2], face_recv_sem.at[2], {"mcol": j_next})
    zface = remote(zhigh, zrecv, face_send_sem.at[3], face_recv_sem.at[3], {"mrow": i_next})
    yface.start()
    zface.start()

    xface_up.wait()
    xface_down.wait()

    def stage(step, inner):
        first = pl.multiple_of(2 * step, 2)
        place = pl.ds(pl.multiple_of(16 * step, 16), 16)
        sources = (
            (mbuf[0, pl.ds(first, 2), 0 : CY // 2, :], xrecv_low[pl.ds(first, 2)]),
            (mbuf[CX - 1, pl.ds(first, 2), CY // 2 : CY, :], xrecv_high[pl.ds(first, 2)]),
        )
        for part, (mine, theirs) in enumerate(sources):
            mine = mine.astype(F32)
            theirs = theirs.astype(F32)
            for block in range(4):
                lanes = slice((4 * part + block) * CZ, (4 * part + block + 1) * CZ)
                right[place, lanes] = rows_of(mine, block)
                left[place, lanes] = rows_of(theirs, block)
        return inner

    lax.fori_loop(0, K // 2, stage, 0)
    low_part = fold(dot_nt(left[0:ROWS, 0 : 4 * CZ], right[:, 0 : 4 * CZ]))
    high_part = fold(dot_nt(right[:, 4 * CZ : 8 * CZ], left[0:ROWS, 4 * CZ : 8 * CZ]))
    part_send[0, :, 0:K] = low_part
    part_send[1, :, 0:K] = high_part.T
    parts = [
        remote(
            part_send.at[slot],
            part_recv.at[slot],
            part_send_sem.at[slot],
            part_recv_sem.at[slot],
            target,
        )
        for slot, target in enumerate(
            ({"sub": s_prev}, {"sub": s_next}, {"mcol": j_prev}, {"mrow": i_prev})
        )
    ]
    parts[0].start()
    parts[1].start()

    gram = fold(acc[...])

    yface.wait()
    y_part = jnp.zeros((K, K), F32)
    for x in range(CX):
        y_part = y_part + dot_nt(yrecv[x], ylow[x])
    part_send[2, :, 0:K] = y_part
    parts[2].start()
    zface.wait()
    z_low = zrows[:, 0:8, :].reshape(K, ROWS).astype(BF16)
    z_part = fold(dot_tn(zrecv[...].astype(F32), z_low.astype(F32)))
    part_send[3, :, 0:K] = z_part
    parts[3].start()

    for mask in masks:
        mask.wait()
    for part in parts:
        part.wait()

    own_row = (iota((K, K), 0) < live).astype(F32)
    own_col = mask_own[0:1, 0:K]
    diag = (iota((K, K), 0) == iota((K, K), 1)).astype(F32)
    diagonal = (gram + gram.T) * own_row * own_col + diag * (1.0 - own_row)

    def finish(block, slot, present):
        kept = own_row * mask_recv[slot, 0:1, 0:K]
        return -block * (kept * jnp.where(present, 1.0, 0.0))

    x_low = finish(low_part.T + part_recv[1, :, 0:K], 0, sub > 0)
    x_high = finish(high_part + part_recv[0, :, 0:K], 1, sub < SUB - 1)
    y_low = finish(y_part.T, 2, mcol > 0)
    y_high = finish(part_recv[2, :, 0:K], 3, mcol < mcols - 1)
    z_lower = finish(z_part.T, 4, mrow > 0)
    z_high = finish(part_recv[3, :, 0:K], 5, mrow < mrows - 1)
    own_out[...] = jnp.concatenate(
        [diagonal, x_high, y_high, z_high, x_low, y_low, z_lower, jnp.zeros((K, K), F32)], axis=1
    )

    head = (mrow == 0) & (mcol == 0)
    second = (mrow == 0) & (mcol == 1)
    third = (mrow == 1) & (mcol == 0)

    @pl.when(head)
    def _():
        gathered[sub] = own_out[:, 0 : 4 * K]

    def cross(which, target):
        return remote(
            gathered.at[sub],
            gathered.at[sub],
            cross_send_sem.at[which],
            line_recv_sem.at[0],
            target,
        )

    def line(step):
        return remote(
            gathered.at[sub],
            gathered.at[sub],
            line_send_sem.at[step],
            line_recv_sem.at[step],
            {"sub": lax.rem(sub + step, SUB)},
        )

    def arrival(step):
        source = lax.rem(sub + SUB - step, SUB)
        return remote(
            gathered.at[source],
            gathered.at[source],
            line_send_sem.at[step],
            line_recv_sem.at[step],
            {"sub": source},
        )

    @pl.when(head)
    def _():
        cross(0, {"mcol": j_next}).start()
        cross(1, {"mrow": i_next}).start()

    @pl.when(second | third)
    def _():
        remote(
            gathered.at[sub],
            gathered.at[sub],
            cross_send_sem.at[0],
            line_recv_sem.at[0],
            {"mcol": j_prev},
        ).wait_recv()

    @pl.when(head | second | third)
    def _():
        for step in range(1, SUB):
            line(step).start()
        for step in range(1, SUB):
            arrival(step).wait_recv()
        for step in range(1, SUB):
            line(step).wait_send()

    @pl.when(head)
    def _():
        cross(0, {"mcol": j_next}).wait_send()
        cross(1, {"mrow": i_next}).wait_send()


def factor_kernel(own, gathered, out, rows, xin, xall):
    mrow = lax.axis_index("mrow")
    mcol = lax.axis_index("mcol")
    sub = lax.axis_index("sub")
    mrows = lax.axis_size("mrow")
    mcols = lax.axis_size("mcol")
    position = (mrow * mcols + mcol) * SUB + sub
    head = (mrow == 0) & (mcol == 0)
    second = (mrow == 0) & (mcol == 1)
    third = (mrow == 1) & (mcol == 0)
    odd = lax.rem(sub, 2) == 1

    out[...] = jnp.zeros_like(out)

    def tile(index):
        return pl.ds(pl.multiple_of(index * 128, 128), 128)

    def block(index):
        return own[:, index * K : (index + 1) * K]

    empty = jnp.zeros((K, K), F32)

    @pl.when(jnp.logical_not(head))
    def _():
        diagonal, x_high, y_high, z_high, x_low, y_low, z_low = (block(n) for n in range(7))
        here = position // 2
        pair_even = jnp.concatenate([diagonal, x_high], axis=1)
        pair_odd = jnp.concatenate([x_low, diagonal], axis=1)
        out[:, tile(here)] = jnp.where(odd, pair_odd, pair_even)

        @pl.when(odd & (sub < SUB - 1))
        def _():
            out[:, tile(here + 1)] = jnp.concatenate([x_high, empty], axis=1)

        @pl.when(jnp.logical_not(odd) & (sub > 0))
        def _():
            out[:, tile(here - 1)] = jnp.concatenate([empty, x_low], axis=1)

        def either(value):
            return jnp.where(
                odd,
                jnp.concatenate([empty, value], axis=1),
                jnp.concatenate([value, empty], axis=1),
            )

        for value, present, stride in (
            (y_high, mcol < mcols - 1, SUB // 2),
            (y_low, (mcol > 0) & jnp.logical_not(second), -(SUB // 2)),
            (z_high, mrow < mrows - 1, mcols * SUB // 2),
            (z_low, (mrow > 0) & jnp.logical_not(third), -(mcols * SUB // 2)),
        ):

            @pl.when(present)
            def _():
                out[:, tile(here + stride)] = either(value)

    @pl.when(head | second | third)
    def _():
        lane = iota((K, 8 * K), 1) >> 6

        def placed(index):
            values = gathered[index]
            first = jnp.concatenate([values[:, 2 * K : 3 * K]] * 8, axis=1)
            other = jnp.concatenate([values[:, 3 * K : 4 * K]] * 8, axis=1)
            first = jnp.where(lane == index, first, 0.0)
            other = jnp.where(lane == index, other, 0.0)
            return jnp.concatenate([first, other], axis=1)

        xin[...] = placed(0)

        def step(index, pivot):
            state = jnp.concatenate([pivot, gathered[index][:, K : 2 * K]], axis=1)
            inverse = (iota((K, 128), 0) == iota((K, 128), 1)).astype(F32)
            row_ids = iota((K, 1), 0)
            for col in range(K):
                top = (col // 8) * 8
                scale = lax.rsqrt(state[col : col + 1, col : col + 1])
                line = state[col : col + 1, :] * scale
                line_inverse = inverse[col : col + 1, :] * scale
                rows[index, col : col + 1, 0:128] = line
                rows[index, col : col + 1, 128:256] = line_inverse
                factor = state[:, col : col + 1] * scale
                factor = jnp.where(row_ids > col, factor, 0.0)
                state = state - factor * line
                inverse = inverse - factor * line_inverse
            coupled = rows[index, :, K : 2 * K]
            solved = dot_nn(rows[index, :, 2 * K : 3 * K], xin[...], HI)
            xall[pl.ds(pl.multiple_of(index * K, K), K), :] = solved
            following = jnp.minimum(index + 1, SUB - 1)
            xin[...] = placed(following) - dot_tn(coupled, solved, HI)
            return gathered[following][:, 0:K] - dot_tn(coupled, coupled, HI)

        lax.fori_loop(0, SUB, step, gathered[0][:, 0:K])

    @pl.when(head)
    def _():
        upper = iota((K, K), 0) <= iota((K, K), 1)
        mine = jnp.where(upper, rows[sub, :, 0:K], 0.0).T
        before = rows[jnp.maximum(sub - 1, 0), :, K : 2 * K].T
        here = sub // 2
        out[:, tile(here)] = jnp.where(
            odd,
            jnp.concatenate([before, mine], axis=1),
            jnp.concatenate([mine, empty], axis=1),
        )

        @pl.when(jnp.logical_not(odd) & (sub > 0))
        def _():
            out[:, tile(here - 1)] = jnp.concatenate([empty, before], axis=1)

    @pl.when(second | third)
    def _():
        which = jnp.where(third, SUB, 0) + sub
        mine = xall[:, tile(which // 2)]
        mine = jnp.where(odd, pltpu.roll(mine, K, 1), mine)
        out[:, 0 : 8 * K] = mine.T[0:K, :]
        product = dot_tn(mine, xall[...], HI)[0:K]
        out[:, 8 * K : 16 * K] -= product[:, 0 : 8 * K]
        far = mcols * SUB * K
        out[:, far : far + 8 * K] -= product[:, 8 * K : 16 * K]


def shards(deflation, reaction, vector_counts):
    vmem = pl.BlockSpec(memory_space=pltpu.VMEM)
    own, gathered = pl.pallas_call(
        assemble_kernel,
        out_shape=(
            jax.ShapeDtypeStruct((K, 8 * K), F32),
            jax.ShapeDtypeStruct((SUB, K, 4 * K), F32),
        ),
        in_specs=[
            pl.BlockSpec(memory_space=pl.ANY),
            vmem,
            pl.BlockSpec(memory_space=pltpu.SMEM),
        ],
        out_specs=(vmem, vmem),
        scratch_shapes=[
            pltpu.VMEM((CX + 1, K, CY, CZ), BF16),
            pltpu.VMEM((ROWS + 16, 8 * CZ), BF16),
            pltpu.VMEM((ROWS, 8 * CZ), BF16),
            pltpu.VMEM((ROWS, ROWS), F32),
            pltpu.VMEM((CX, CY, CZ), F32),
            pltpu.VMEM((CX, 16, ROWS), F32),
            pltpu.VMEM((CX, K, CZ), BF16),
            pltpu.VMEM((CX, K, CZ), BF16),
            pltpu.VMEM((CX, K, CZ), BF16),
            pltpu.VMEM((K, ROWS), BF16),
            pltpu.VMEM((K, ROWS), BF16),
            pltpu.VMEM((K, CY // 2, CZ), BF16),
            pltpu.VMEM((K, CY // 2, CZ), BF16),
            pltpu.VMEM((8, 128), F32),
            pltpu.VMEM((6, 8, 128), F32),
            pltpu.VMEM((4, K, 128), F32),
            pltpu.VMEM((4, K, 128), F32),
            pltpu.SemaphoreType.DMA((CX,)),
            pltpu.SemaphoreType.DMA((6,)),
            pltpu.SemaphoreType.DMA((6,)),
            pltpu.SemaphoreType.DMA((4,)),
            pltpu.SemaphoreType.DMA((4,)),
            pltpu.SemaphoreType.DMA((4,)),
            pltpu.SemaphoreType.DMA((4,)),
            pltpu.SemaphoreType.DMA((SUB,)),
            pltpu.SemaphoreType.DMA((2,)),
            pltpu.SemaphoreType.DMA((SUB,)),
        ],
        compiler_params=pltpu.CompilerParams(
            collective_id=0, has_side_effects=True, vmem_limit_bytes=56 * 1024 * 1024
        ),
        name="assemble",
    )(deflation, reaction, vector_counts)
    return pl.pallas_call(
        factor_kernel,
        out_shape=jax.ShapeDtypeStruct((K, 128 * K), F32),
        in_specs=[vmem, vmem],
        out_specs=vmem,
        scratch_shapes=[
            pltpu.VMEM((SUB, K, 256), F32),
            pltpu.VMEM((K, 16 * K), F32),
            pltpu.VMEM((SUB * K, 16 * K), F32),
        ],
        compiler_params=pltpu.CompilerParams(vmem_limit_bytes=56 * 1024 * 1024),
        name="factor",
    )(own, gathered)


def solution(mesh):
    return jax.shard_map(
        shards,
        mesh=mesh,
        in_specs=(
            P(None, "sub", "mcol", "mrow"),
            P("sub", "mcol", "mrow"),
            P(("mrow", "mcol", "sub")),
        ),
        out_specs=P(("mrow", "mcol", "sub"), None),
        check_vma=False,
    )
```

```python
import functools

import jax
import jax.numpy as jnp
from jax import lax
from jax.experimental import pallas as pl
from jax.experimental.pallas import tpu as pltpu
from jax.sharding import PartitionSpec as P

MESH = pl.DeviceIdType.MESH
F32 = jnp.float32
BF16 = jnp.bfloat16
HI = lax.Precision.HIGHEST
K = 64
CX = 8
CY = 64
CZ = 256
ROWS = K * 8
SUB = 8


def dot_nt(a, b, precision=None):
    return lax.dot_general(
        a, b, (((1,), (1,)), ((), ())), precision=precision, preferred_element_type=F32
    )


def dot_nn(a, b, precision=None):
    return lax.dot_general(
        a, b, (((1,), (0,)), ((), ())), precision=precision, preferred_element_type=F32
    )


def dot_tn(a, b, precision=None):
    return lax.dot_general(
        a, b, (((0,), (0,)), ((), ())), precision=precision, preferred_element_type=F32
    )


def iota(shape, axis):
    return lax.broadcasted_iota(jnp.int32, shape, axis)


def fold(product):
    same = (iota(product.shape, 0) & 7) == (iota(product.shape, 1) & 7)
    kept = jnp.where(same, product, 0.0).reshape(K, 8, ROWS).sum(axis=1)
    collect = ((iota((ROWS, K), 0) >> 3) == iota((ROWS, K), 1)).astype(F32)
    return dot_nn(kept, collect, HI)


def assemble_kernel(
    defl,
    react,
    count,
    own_out,
    gathered,
    mbuf,
    left,
    right,
    acc,
    weight,
    zrows,
    ylow,
    yhigh,
    yrecv,
    zhigh,
    zrecv,
    xrecv_low,
    xrecv_high,
    mask_own,
    mask_recv,
    part_send,
    part_recv,
    load_sem,
    mask_send_sem,
    mask_recv_sem,
    face_send_sem,
    face_recv_sem,
    part_send_sem,
    part_recv_sem,
    line_send_sem,
    cross_send_sem,
    line_recv_sem,
):
    mrow = lax.axis_index("mrow")
    mcol = lax.axis_index("mcol")
    sub = lax.axis_index("sub")
    mrows = lax.axis_size("mrow")
    mcols = lax.axis_size("mcol")
    s_next, s_prev = lax.rem(sub + 1, SUB), lax.rem(sub + SUB - 1, SUB)
    j_next, j_prev = lax.rem(mcol + 1, mcols), lax.rem(mcol + mcols - 1, mcols)
    i_next, i_prev = lax.rem(mrow + 1, mrows), lax.rem(mrow + mrows - 1, mrows)

    loads = [
        pltpu.make_async_copy(defl.at[:, x], mbuf.at[x], load_sem.at[x]) for x in range(CX)
    ]
    for load in loads:
        load.start()

    barrier = pltpu.get_barrier_semaphore()
    for step in range(1, SUB):
        pl.semaphore_signal(
            barrier,
            inc=1,
            device_id={"sub": lax.rem(sub + step, SUB)},
            device_id_type=MESH,
        )
    for axis, other in (
        ("mcol", j_next),
        ("mcol", j_prev),
        ("mrow", i_next),
        ("mrow", i_prev),
    ):
        pl.semaphore_signal(barrier, inc=1, device_id={axis: other}, device_id_type=MESH)
    pl.semaphore_wait(barrier, SUB - 1 + 4)

    def remote(src, dst, send, recv, target):
        return pltpu.make_async_remote_copy(
            src_ref=src,
            dst_ref=dst,
            send_sem=send,
            recv_sem=recv,
            device_id=target,
            device_id_type=MESH,
        )

    xface_up = remote(
        defl.at[:, CX - 1, 0 : CY // 2],
        xrecv_low,
        face_send_sem.at[0],
        face_recv_sem.at[0],
        {"sub": s_next},
    )
    xface_down = remote(
        defl.at[:, 0, CY // 2 : CY],
        xrecv_high,
        face_send_sem.at[1],
        face_recv_sem.at[1],
        {"sub": s_prev},
    )
    xface_up.start()
    xface_down.start()

    live = count[0]
    mask_own[...] = (iota((8, 128), 1) < live).astype(F32)
    masks = []
    for slot, target in enumerate(
        (
            {"sub": s_next},
            {"sub": s_prev},
            {"mcol": j_next},
            {"mcol": j_prev},
            {"mrow": i_next},
            {"mrow": i_prev},
        )
    ):
        masks.append(
            remote(
                mask_own,
                mask_recv.at[slot],
                mask_send_sem.at[slot],
                mask_recv_sem.at[slot],
                target,
            )
        )
        masks[-1].start()

    weight[...] = 3.0 + 0.5 * react[...]
    mbuf[CX] = jnp.zeros((K, CY, CZ), BF16)
    acc[...] = jnp.zeros_like(acc)
    part_send[...] = jnp.zeros_like(part_send)
    tail = iota((16, 8 * CZ), 0)
    spot = (tail & 7) * CZ + (tail >> 3) * (CZ - 1)
    left[ROWS : ROWS + 16, :] = (iota((16, 8 * CZ), 1) == spot).astype(F32).astype(BF16)

    group = 4
    last_lane = iota((1, 1, 128), 2) == 127
    last_row = iota((1, 8, 1), 1) == 7

    def flat(value):
        return value.reshape(8 * group, CZ).astype(BF16)

    def stage_group(x, first, row):
        here = mbuf[x, pl.ds(first, group)].astype(F32)
        after_x = mbuf[x + 1, pl.ds(first, group)].astype(F32)
        turned_low = pltpu.roll(here[:, :, 0:128], 127, 2)
        turned_high = pltpu.roll(here[:, :, 128:256], 127, 2)
        after_z = jnp.concatenate(
            [
                jnp.where(last_lane, turned_high, turned_low),
                jnp.where(last_lane, 0.0, turned_high),
            ],
            axis=2,
        )
        turned = [pltpu.roll(here[:, 8 * n : 8 * n + 8, :], 7, 1) for n in range(8)]
        turned.append(jnp.zeros((group, 8, CZ), F32))
        place = pl.ds(row, 8 * group)
        for block in range(8):
            rows = slice(8 * block, 8 * block + 8)
            lanes = slice(block * CZ, (block + 1) * CZ)
            after_y = jnp.where(last_row, turned[block + 1], turned[block])
            half = weight[x, rows][None] * here[:, rows] - after_x[:, rows]
            half = half - after_y - after_z[:, rows]
            left[place, lanes] = flat(half)
            right[place, lanes] = flat(here[:, rows])

    def plane(x, carry):
        @pl.when(x < CX - 1)
        def _():
            pltpu.make_async_copy(
                defl.at[:, x + 1], mbuf.at[x + 1], load_sem.at[x + 1]
            ).wait()

        def part(step, inner):
            for q in range(K // 2 // group):
                first = pl.multiple_of(step * (K // 2) + q * group, group)
                row = pl.multiple_of(step * (K // 2 * 8) + q * group * 8, group * 8)
                stage_group(x, first, row)
            return inner

        lax.fori_loop(0, 2, part, 0)
        product = dot_nt(left[...], right[...])
        acc[...] += product[:ROWS]
        zrows[x] = product[ROWS : ROWS + 16]
        pick_row = iota((K, ROWS), 0) * 8
        pick_low = (iota((K, ROWS), 1) == pick_row).astype(F32).astype(BF16)
        pick_high = (iota((K, ROWS), 1) == pick_row + 7).astype(F32).astype(BF16)
        ylow[x] = dot_nn(pick_low, right[:, 0:CZ]).astype(BF16)
        yhigh[x] = dot_nn(pick_high, right[:, 7 * CZ : 8 * CZ]).astype(BF16)
        return carry

    loads[0].wait()
    lax.fori_loop(0, CX, plane, 0)

    zhigh[...] = zrows[:, 8:16, :].reshape(K, ROWS).astype(BF16)
    yface = remote(yhigh, yrecv, face_send_sem.at[2], face_recv_sem.at[2], {"mcol": j_next})
    zface = remote(zhigh, zrecv, face_send_sem.at[3], face_recv_sem.at[3], {"mrow": i_next})
    yface.start()
    zface.start()

    xface_up.wait()
    xface_down.wait()

    def stage(step, inner):
        for q in range(2):
            first = pl.multiple_of(8 * step + q * group, group)
            place = pl.ds(pl.multiple_of(64 * step + q * group * 8, group * 8), group * 8)
            chosen = pl.ds(first, group)
            sources = (
                (mbuf[0, chosen, 0 : CY // 2, :], xrecv_low[chosen]),
                (mbuf[CX - 1, chosen, CY // 2 : CY, :], xrecv_high[chosen]),
            )
            for part, (mine, theirs) in enumerate(sources):
                mine = mine.astype(F32)
                theirs = theirs.astype(F32)
                for block in range(4):
                    rows = slice(8 * block, 8 * block + 8)
                    lanes = slice((4 * part + block) * CZ, (4 * part + block + 1) * CZ)
                    right[place, lanes] = flat(mine[:, rows])
                    left[place, lanes] = flat(theirs[:, rows])
        return inner

    lax.fori_loop(0, K // 8, stage, 0)
    low_part = fold(dot_nt(left[0:ROWS, 0 : 4 * CZ], right[:, 0 : 4 * CZ]))
    high_part = fold(dot_nt(right[:, 4 * CZ : 8 * CZ], left[0:ROWS, 4 * CZ : 8 * CZ]))
    part_send[0, :, 0:K] = low_part
    part_send[1, :, 0:K] = high_part.T
    parts = [
        remote(
            part_send.at[slot],
            part_recv.at[slot],
            part_send_sem.at[slot],
            part_recv_sem.at[slot],
            target,
        )
        for slot, target in enumerate(
            ({"sub": s_prev}, {"sub": s_next}, {"mcol": j_prev}, {"mrow": i_prev})
        )
    ]
    parts[0].start()
    parts[1].start()

    gram = fold(acc[...])

    yface.wait()
    y_part = jnp.zeros((K, K), F32)
    for x in range(CX):
        y_part = y_part + dot_nt(yrecv[x], ylow[x])
    part_send[2, :, 0:K] = y_part
    parts[2].start()
    zface.wait()
    z_low = zrows[:, 0:8, :].reshape(K, ROWS).astype(BF16)
    z_part = fold(dot_tn(zrecv[...].astype(F32), z_low.astype(F32)))
    part_send[3, :, 0:K] = z_part
    parts[3].start()

    for mask in masks:
        mask.wait()
    for part in parts:
        part.wait()

    own_row = (iota((K, K), 0) < live).astype(F32)
    own_col = mask_own[0:1, 0:K]
    diag = (iota((K, K), 0) == iota((K, K), 1)).astype(F32)
    diagonal = (gram + gram.T) * own_row * own_col + diag * (1.0 - own_row)

    def finish(block, slot, present):
        kept = own_row * mask_recv[slot, 0:1, 0:K]
        return -block * (kept * jnp.where(present, 1.0, 0.0))

    x_low = finish(low_part.T + part_recv[1, :, 0:K], 0, sub > 0)
    x_high = finish(high_part + part_recv[0, :, 0:K], 1, sub < SUB - 1)
    y_low = finish(y_part.T, 2, mcol > 0)
    y_high = finish(part_recv[2, :, 0:K], 3, mcol < mcols - 1)
    z_lower = finish(z_part.T, 4, mrow > 0)
    z_high = finish(part_recv[3, :, 0:K], 5, mrow < mrows - 1)
    own_out[...] = jnp.concatenate(
        [diagonal, x_high, y_high, z_high, x_low, y_low, z_lower, jnp.zeros((K, K), F32)], axis=1
    )

    head = (mrow == 0) & (mcol == 0)
    second = (mrow == 0) & (mcol == 1)
    third = (mrow == 1) & (mcol == 0)

    @pl.when(head)
    def _():
        gathered[sub] = own_out[:, 0 : 4 * K]

    def cross(which, target):
        return remote(
            gathered.at[sub],
            gathered.at[sub],
            cross_send_sem.at[which],
            line_recv_sem.at[0],
            target,
        )

    def line(step):
        return remote(
            gathered.at[sub],
            gathered.at[sub],
            line_send_sem.at[step],
            line_recv_sem.at[step],
            {"sub": lax.rem(sub + step, SUB)},
        )

    def arrival(step):
        source = lax.rem(sub + SUB - step, SUB)
        return remote(
            gathered.at[source],
            gathered.at[source],
            line_send_sem.at[step],
            line_recv_sem.at[step],
            {"sub": source},
        )

    @pl.when(head)
    def _():
        cross(0, {"mcol": j_next}).start()
        cross(1, {"mrow": i_next}).start()

    @pl.when(second | third)
    def _():
        remote(
            gathered.at[sub],
            gathered.at[sub],
            cross_send_sem.at[0],
            line_recv_sem.at[0],
            {"mcol": j_prev},
        ).wait_recv()

    @pl.when(head | second | third)
    def _():
        for step in range(1, SUB):
            line(step).start()
        for step in range(1, SUB):
            arrival(step).wait_recv()
        for step in range(1, SUB):
            line(step).wait_send()

    @pl.when(head)
    def _():
        cross(0, {"mcol": j_next}).wait_send()
        cross(1, {"mrow": i_next}).wait_send()


def factor_kernel(own, gathered, out, rows, xin, xall):
    mrow = lax.axis_index("mrow")
    mcol = lax.axis_index("mcol")
    sub = lax.axis_index("sub")
    mrows = lax.axis_size("mrow")
    mcols = lax.axis_size("mcol")
    position = (mrow * mcols + mcol) * SUB + sub
    head = (mrow == 0) & (mcol == 0)
    second = (mrow == 0) & (mcol == 1)
    third = (mrow == 1) & (mcol == 0)
    odd = lax.rem(sub, 2) == 1

    out[...] = jnp.zeros_like(out)

    def tile(index):
        return pl.ds(pl.multiple_of(index * 128, 128), 128)

    def block(index):
        return own[:, index * K : (index + 1) * K]

    empty = jnp.zeros((K, K), F32)

    @pl.when(jnp.logical_not(head))
    def _():
        diagonal, x_high, y_high, z_high, x_low, y_low, z_low = (block(n) for n in range(7))
        here = position // 2
        pair_even = jnp.concatenate([diagonal, x_high], axis=1)
        pair_odd = jnp.concatenate([x_low, diagonal], axis=1)
        out[:, tile(here)] = jnp.where(odd, pair_odd, pair_even)

        @pl.when(odd & (sub < SUB - 1))
        def _():
            out[:, tile(here + 1)] = jnp.concatenate([x_high, empty], axis=1)

        @pl.when(jnp.logical_not(odd) & (sub > 0))
        def _():
            out[:, tile(here - 1)] = jnp.concatenate([empty, x_low], axis=1)

        def either(value):
            return jnp.where(
                odd,
                jnp.concatenate([empty, value], axis=1),
                jnp.concatenate([value, empty], axis=1),
            )

        for value, present, stride in (
            (y_high, mcol < mcols - 1, SUB // 2),
            (y_low, (mcol > 0) & jnp.logical_not(second), -(SUB // 2)),
            (z_high, mrow < mrows - 1, mcols * SUB // 2),
            (z_low, (mrow > 0) & jnp.logical_not(third), -(mcols * SUB // 2)),
        ):

            @pl.when(present)
            def _():
                out[:, tile(here + stride)] = either(value)

    @pl.when(head | second | third)
    def _():
        lane = iota((K, 8 * K), 1) >> 6

        def placed(index):
            values = gathered[index]
            first = jnp.concatenate([values[:, 2 * K : 3 * K]] * 8, axis=1)
            other = jnp.concatenate([values[:, 3 * K : 4 * K]] * 8, axis=1)
            first = jnp.where(lane == index, first, 0.0)
            other = jnp.where(lane == index, other, 0.0)
            return jnp.concatenate([first, other], axis=1)

        xin[...] = placed(0)

        def eliminate(index, pivot):
            coupling = gathered[index][:, K : 2 * K]
            unit = (iota((K, 128), 0) == iota((K, 128), 1)).astype(F32)
            state = jnp.concatenate([pivot, coupling], axis=1)
            state = [state[8 * n : 8 * n + 8] for n in range(8)]
            inverse = [unit[8 * n : 8 * n + 8] for n in range(8)]
            for now in range(8):
                columns = {
                    n: [
                        jnp.broadcast_to(state[n][:, 8 * now + c : 8 * now + c + 1], (8, 128))
                        for c in range(8)
                    ]
                    for n in range(now, 8)
                }
                lower = {}
                scale = []
                for c in range(8):
                    value = columns[now][c][c : c + 1]
                    for k in range(c):
                        value = value - lower[c, k] * lower[c, k]
                    scale.append(lax.rsqrt(value))
                    for r in range(c + 1, 8):
                        value = columns[now][c][r : r + 1]
                        for k in range(c):
                            value = value - lower[r, k] * lower[c, k]
                        lower[r, c] = value * scale[c]
                lines, lines_inverse = [], []
                for c in range(8):
                    line = state[now][c : c + 1]
                    line_inverse = inverse[now][c : c + 1]
                    for k in range(c):
                        line = line - lower[c, k] * lines[k]
                        line_inverse = line_inverse - lower[c, k] * lines_inverse[k]
                    lines.append(line * scale[c])
                    lines_inverse.append(line_inverse * scale[c])
                    at = 8 * now + c
                    rows[index, at : at + 1, 0:128] = lines[c]
                    rows[index, at : at + 1, 128:256] = lines_inverse[c]
                for n in range(now + 1, 8):
                    factors = []
                    for c in range(8):
                        factor = columns[n][c]
                        for k in range(c):
                            factor = factor - factors[k] * lower[c, k]
                        factors.append(factor * scale[c])
                    for c in range(8):
                        state[n] = state[n] - factors[c] * lines[c]
                        inverse[n] = inverse[n] - factors[c] * lines_inverse[c]

        def step(index, pivot):
            eliminate(index, pivot)
            coupled = rows[index, :, K : 2 * K]
            solved = dot_nn(rows[index, :, 2 * K : 3 * K], xin[...], HI)
            xall[pl.ds(pl.multiple_of(index * K, K), K), :] = solved
            following = jnp.minimum(index + 1, SUB - 1)
            xin[...] = placed(following) - dot_tn(coupled, solved, HI)
            return gathered[following][:, 0:K] - dot_tn(coupled, coupled, HI)

        lax.fori_loop(0, SUB, step, gathered[0][:, 0:K])

    @pl.when(head)
    def _():
        upper = iota((K, K), 0) <= iota((K, K), 1)
        mine = jnp.where(upper, rows[sub, :, 0:K], 0.0).T
        before = rows[jnp.maximum(sub - 1, 0), :, K : 2 * K].T
        here = sub // 2
        out[:, tile(here)] = jnp.where(
            odd,
            jnp.concatenate([before, mine], axis=1),
            jnp.concatenate([mine, empty], axis=1),
        )

        @pl.when(jnp.logical_not(odd) & (sub > 0))
        def _():
            out[:, tile(here - 1)] = jnp.concatenate([empty, before], axis=1)

    @pl.when(second | third)
    def _():
        which = jnp.where(third, SUB, 0) + sub
        mine = xall[:, tile(which // 2)]
        mine = jnp.where(odd, pltpu.roll(mine, K, 1), mine)
        out[:, 0 : 8 * K] = mine.T[0:K, :]
        product = dot_tn(mine, xall[...], HI)[0:K]
        out[:, 8 * K : 16 * K] -= product[:, 0 : 8 * K]
        far = mcols * SUB * K
        out[:, far : far + 8 * K] -= product[:, 8 * K : 16 * K]


def shards(deflation, reaction, vector_counts):
    vmem = pl.BlockSpec(memory_space=pltpu.VMEM)
    own, gathered = pl.pallas_call(
        assemble_kernel,
        out_shape=(
            jax.ShapeDtypeStruct((K, 8 * K), F32),
            jax.ShapeDtypeStruct((SUB, K, 4 * K), F32),
        ),
        in_specs=[
            pl.BlockSpec(memory_space=pl.ANY),
            vmem,
            pl.BlockSpec(memory_space=pltpu.SMEM),
        ],
        out_specs=(vmem, vmem),
        scratch_shapes=[
            pltpu.VMEM((CX + 1, K, CY, CZ), BF16),
            pltpu.VMEM((ROWS + 16, 8 * CZ), BF16),
            pltpu.VMEM((ROWS, 8 * CZ), BF16),
            pltpu.VMEM((ROWS, ROWS), F32),
            pltpu.VMEM((CX, CY, CZ), F32),
            pltpu.VMEM((CX, 16, ROWS), F32),
            pltpu.VMEM((CX, K, CZ), BF16),
            pltpu.VMEM((CX, K, CZ), BF16),
            pltpu.VMEM((CX, K, CZ), BF16),
            pltpu.VMEM((K, ROWS), BF16),
            pltpu.VMEM((K, ROWS), BF16),
            pltpu.VMEM((K, CY // 2, CZ), BF16),
            pltpu.VMEM((K, CY // 2, CZ), BF16),
            pltpu.VMEM((8, 128), F32),
            pltpu.VMEM((6, 8, 128), F32),
            pltpu.VMEM((4, K, 128), F32),
            pltpu.VMEM((4, K, 128), F32),
            pltpu.SemaphoreType.DMA((CX,)),
            pltpu.SemaphoreType.DMA((6,)),
            pltpu.SemaphoreType.DMA((6,)),
            pltpu.SemaphoreType.DMA((4,)),
            pltpu.SemaphoreType.DMA((4,)),
            pltpu.SemaphoreType.DMA((4,)),
            pltpu.SemaphoreType.DMA((4,)),
            pltpu.SemaphoreType.DMA((SUB,)),
            pltpu.SemaphoreType.DMA((2,)),
            pltpu.SemaphoreType.DMA((SUB,)),
        ],
        compiler_params=pltpu.CompilerParams(
            collective_id=0, has_side_effects=True, vmem_limit_bytes=56 * 1024 * 1024
        ),
        name="assemble",
    )(deflation, reaction, vector_counts)
    return pl.pallas_call(
        factor_kernel,
        out_shape=jax.ShapeDtypeStruct((K, 128 * K), F32),
        in_specs=[vmem, vmem],
        out_specs=vmem,
        scratch_shapes=[
            pltpu.VMEM((SUB, K, 256), F32),
            pltpu.VMEM((K, 16 * K), F32),
            pltpu.VMEM((SUB * K, 16 * K), F32),
        ],
        compiler_params=pltpu.CompilerParams(vmem_limit_bytes=56 * 1024 * 1024),
        name="factor",
    )(own, gathered)


def solution(mesh):
    return jax.shard_map(
        shards,
        mesh=mesh,
        in_specs=(
            P(None, "sub", "mcol", "mrow"),
            P("sub", "mcol", "mrow"),
            P(("mrow", "mcol", "sub")),
        ),
        out_specs=P(("mrow", "mcol", "sub"), None),
        check_vma=False,
    )
```

```python
import functools

import jax
import jax.numpy as jnp
from jax import lax
from jax.experimental import pallas as pl
from jax.experimental.pallas import tpu as pltpu
from jax.sharding import PartitionSpec as P

MESH = pl.DeviceIdType.MESH
F32 = jnp.float32
BF16 = jnp.bfloat16
HI = lax.Precision.HIGHEST
K = 64
CX = 8
CY = 64
CZ = 256
ROWS = K * 8
SUB = 8
EARLY = 6


def dot_nt(a, b, precision=None):
    return lax.dot_general(
        a, b, (((1,), (1,)), ((), ())), precision=precision, preferred_element_type=F32
    )


def dot_nn(a, b, precision=None):
    return lax.dot_general(
        a, b, (((1,), (0,)), ((), ())), precision=precision, preferred_element_type=F32
    )


def dot_tn(a, b, precision=None):
    return lax.dot_general(
        a, b, (((0,), (0,)), ((), ())), precision=precision, preferred_element_type=F32
    )


def iota(shape, axis):
    return lax.broadcasted_iota(jnp.int32, shape, axis)


def fold(product):
    same = (iota(product.shape, 0) & 7) == (iota(product.shape, 1) & 7)
    kept = jnp.where(same, product, 0.0).reshape(K, 8, ROWS).sum(axis=1)
    collect = ((iota((ROWS, K), 0) >> 3) == iota((ROWS, K), 1)).astype(F32)
    return dot_nn(kept, collect, HI)


def assemble_kernel(
    defl,
    react,
    count,
    own_out,
    factor_out,
    product_out,
    mbuf,
    left,
    right,
    acc,
    weight,
    zrows,
    yedge,
    ylow,
    yhigh,
    yrecv,
    zrecv,
    xrecv_low,
    xrecv_high,
    mask_own,
    mask_recv,
    part_send,
    part_recv,
    chain,
    border,
    pivots,
    solver,
    xin,
    xall,
    load_sem,
    mask_send_sem,
    mask_recv_sem,
    face_send_sem,
    face_recv_sem,
    y_send_sem,
    y_recv_sem,
    z_send_sem,
    z_recv_sem,
    part_send_sem,
    part_recv_sem,
    chain_send_sem,
    chain_recv_sem,
    border_send_sem,
    border_recv_sem,
    cross_send_sem,
    solver_send_sem,
    solver_recv_sem,
):
    mrow = lax.axis_index("mrow")
    mcol = lax.axis_index("mcol")
    sub = lax.axis_index("sub")
    mrows = lax.axis_size("mrow")
    mcols = lax.axis_size("mcol")
    s_next, s_prev = lax.rem(sub + 1, SUB), lax.rem(sub + SUB - 1, SUB)
    j_next, j_prev = lax.rem(mcol + 1, mcols), lax.rem(mcol + mcols - 1, mcols)
    i_next, i_prev = lax.rem(mrow + 1, mrows), lax.rem(mrow + mrows - 1, mrows)
    head = (mrow == 0) & (mcol == 0)
    second = (mrow == 0) & (mcol == 1)
    third = (mrow == 1) & (mcol == 0)

    loads = [
        pltpu.make_async_copy(defl.at[:, x], mbuf.at[x], load_sem.at[x]) for x in range(CX)
    ]
    for load in loads:
        load.start()

    barrier = pltpu.get_barrier_semaphore()
    for step in range(1, SUB):
        pl.semaphore_signal(
            barrier,
            inc=1,
            device_id={"sub": lax.rem(sub + step, SUB)},
            device_id_type=MESH,
        )
    for axis, other in (
        ("mcol", j_next),
        ("mcol", j_prev),
        ("mrow", i_next),
        ("mrow", i_prev),
    ):
        pl.semaphore_signal(barrier, inc=1, device_id={axis: other}, device_id_type=MESH)

    live = count[0]
    mask_own[...] = (iota((8, 128), 1) < live).astype(F32)
    weight[...] = 3.0 + 0.5 * react[...]
    mbuf[CX] = jnp.zeros((K, CY, CZ), BF16)
    acc[...] = jnp.zeros_like(acc)
    part_send[...] = jnp.zeros_like(part_send)
    tail = iota((16, 8 * CZ), 0)
    spot = (tail & 7) * CZ + (tail >> 3) * (CZ - 1)
    left[ROWS : ROWS + 16, :] = (iota((16, 8 * CZ), 1) == spot).astype(F32).astype(BF16)

    pl.semaphore_wait(barrier, SUB - 1 + 4)

    def remote(src, dst, send, recv, target):
        return pltpu.make_async_remote_copy(
            src_ref=src,
            dst_ref=dst,
            send_sem=send,
            recv_sem=recv,
            device_id=target,
            device_id_type=MESH,
        )

    xface_up = remote(
        defl.at[:, CX - 1, 0 : CY // 2],
        xrecv_low,
        face_send_sem.at[0],
        face_recv_sem.at[0],
        {"sub": s_next},
    )
    xface_down = remote(
        defl.at[:, 0, CY // 2 : CY],
        xrecv_high,
        face_send_sem.at[1],
        face_recv_sem.at[1],
        {"sub": s_prev},
    )
    xface_up.start()
    xface_down.start()

    masks = []
    for slot, target in enumerate(
        (
            {"sub": s_next},
            {"sub": s_prev},
            {"mcol": j_next},
            {"mcol": j_prev},
            {"mrow": i_next},
            {"mrow": i_prev},
        )
    ):
        masks.append(
            remote(
                mask_own,
                mask_recv.at[slot],
                mask_send_sem.at[slot],
                mask_recv_sem.at[slot],
                target,
            )
        )
        masks[-1].start()

    group = 4
    last_lane = iota((1, 1, 128), 2) == 127
    last_row = iota((1, 8, 1), 1) == 7

    def flat(value):
        return value.reshape(8 * group, CZ).astype(BF16)

    def stage_group(x, first, row):
        here = mbuf[x, pl.ds(first, group)].astype(F32)
        after_x = mbuf[x + 1, pl.ds(first, group)].astype(F32)
        turned_low = pltpu.roll(here[:, :, 0:128], 127, 2)
        turned_high = pltpu.roll(here[:, :, 128:256], 127, 2)
        after_z = jnp.concatenate(
            [
                jnp.where(last_lane, turned_high, turned_low),
                jnp.where(last_lane, 0.0, turned_high),
            ],
            axis=2,
        )
        turned = [pltpu.roll(here[:, 8 * n : 8 * n + 8, :], 7, 1) for n in range(8)]
        turned.append(jnp.zeros((group, 8, CZ), F32))
        place = pl.ds(row, 8 * group)
        for block in range(8):
            part = slice(8 * block, 8 * block + 8)
            lanes = slice(block * CZ, (block + 1) * CZ)
            after_y = jnp.where(last_row, turned[block + 1], turned[block])
            half = weight[x, part][None] * here[:, part] - after_x[:, part]
            half = half - after_y - after_z[:, part]
            left[place, lanes] = flat(half)
            right[place, lanes] = flat(here[:, part])
        for n in range(group):
            yedge[0, pl.ds(first + n, 1), :] = here[n, 0:1, :]
            yedge[1, pl.ds(first + n, 1), :] = here[n, CY - 1 : CY, :]

    def y_face(x):
        return remote(
            yhigh.at[x], yrecv.at[x], y_send_sem.at[x], y_recv_sem.at[x], {"mcol": j_next}
        )

    def z_face(x):
        return remote(
            zrows.at[x, pl.ds(8, 8)],
            zrecv.at[x],
            z_send_sem.at[x],
            z_recv_sem.at[x],
            {"mrow": i_next},
        )

    def plane(x, carry):
        @pl.when(x < EARLY)
        def _():
            pltpu.make_async_copy(
                defl.at[:, x + 1], mbuf.at[x + 1], load_sem.at[x + 1]
            ).wait()

        def part(step, inner):
            for q in range(K // 2 // group):
                first = pl.multiple_of(step * (K // 2) + q * group, group)
                row = pl.multiple_of(step * (K // 2 * 8) + q * group * 8, group * 8)
                stage_group(x, first, row)
            return inner

        lax.fori_loop(0, 2, part, 0)
        ylow[x] = yedge[0].astype(BF16)
        yhigh[x] = yedge[1].astype(BF16)
        y_face(x).start()
        product = dot_nt(left[...], right[...])
        acc[...] += product[:ROWS]
        zrows[x] = product[ROWS : ROWS + 16]
        z_face(x).start()
        return carry

    loads[0].wait()
    lax.fori_loop(0, EARLY, plane, 0)

    for load in loads[EARLY + 1 :]:
        load.wait()
    xface_up.wait()
    xface_down.wait()

    def stage(step, inner):
        for q in range(2):
            first = pl.multiple_of(8 * step + q * group, group)
            place = pl.ds(pl.multiple_of(64 * step + q * group * 8, group * 8), group * 8)
            chosen = pl.ds(first, group)
            sources = (
                (mbuf[0, chosen, 0 : CY // 2, :], xrecv_low[chosen]),
                (last_half[chosen], xrecv_high[chosen]),
            )
            for which, (mine, theirs) in enumerate(sources):
                mine = mine.astype(F32)
                theirs = theirs.astype(F32)
                for block in range(4):
                    part = slice(8 * block, 8 * block + 8)
                    lanes = slice((4 * which + block) * CZ, (4 * which + block + 1) * CZ)
                    right[place, lanes] = flat(mine[:, part])
                    left[place, lanes] = flat(theirs[:, part])
        return inner

    last_half = mbuf.at[CX - 1, :, CY // 2 : CY, :]
    lax.fori_loop(0, K // 8, stage, 0)
    low_part = fold(dot_nt(left[0:ROWS, 0 : 4 * CZ], right[:, 0 : 4 * CZ]))
    high_part = fold(dot_nt(right[:, 4 * CZ : 8 * CZ], left[0:ROWS, 4 * CZ : 8 * CZ]))
    part_send[0, :, 0:K] = low_part
    part_send[1, :, 0:K] = high_part.T
    parts = [
        remote(
            part_send.at[slot],
            part_recv.at[slot],
            part_send_sem.at[slot],
            part_recv_sem.at[slot],
            target,
        )
        for slot, target in enumerate(
            ({"sub": s_prev}, {"sub": s_next}, {"mcol": j_prev}, {"mrow": i_prev})
        )
    ]
    parts[0].start()
    parts[1].start()

    lax.fori_loop(EARLY, CX, plane, 0)

    own_row = (iota((K, K), 0) < live).astype(F32)
    own_col = mask_own[0:1, 0:K]
    diag = (iota((K, K), 0) == iota((K, K), 1)).astype(F32)

    def finish(block, slot, present):
        kept = own_row * mask_recv[slot, 0:1, 0:K]
        return -block * (kept * jnp.where(present, 1.0, 0.0))

    gram = fold(acc[...])
    diagonal = (gram + gram.T) * own_row * own_col + diag * (1.0 - own_row)
    for mask in masks:
        mask.wait()
    parts[0].wait()
    parts[1].wait()
    x_low = finish(low_part.T + part_recv[1, :, 0:K], 0, sub > 0)
    x_high = finish(high_part + part_recv[0, :, 0:K], 1, sub < SUB - 1)
    own_out[:, 0 : 2 * K] = jnp.concatenate([diagonal, x_high], axis=1)

    def cross(buffer, recv, which):
        return remote(
            buffer.at[sub],
            buffer.at[sub],
            cross_send_sem.at[which],
            recv.at[sub],
            ({"mcol": j_next}, {"mrow": i_next})[which],
        )

    def line(buffer, send, recv, step):
        return remote(
            buffer.at[sub],
            buffer.at[sub],
            send.at[step],
            recv.at[sub],
            {"sub": lax.rem(sub + step, SUB)},
        )

    def landed(buffer, recv, slot):
        return remote(
            buffer.at[slot],
            buffer.at[slot],
            cross_send_sem.at[0],
            recv.at[slot],
            {"mcol": j_next},
        )

    @pl.when(head)
    def _():
        chain[sub] = jnp.concatenate([diagonal, x_high], axis=1)
        for step in range(1, SUB):
            line(chain, chain_send_sem, chain_recv_sem, step).start()

    for x in range(CX):
        y_face(x).wait()
        z_face(x).wait()
    y_part = dot_nt(
        jnp.concatenate([yrecv[x] for x in range(CX)], axis=1),
        jnp.concatenate([ylow[x] for x in range(CX)], axis=1),
    )
    part_send[2, :, 0:K] = y_part
    parts[2].start()
    z_low = zrows[:, 0:8, :].reshape(K, ROWS)
    z_part = fold(dot_tn(zrecv[...].reshape(K, ROWS), z_low))
    part_send[3, :, 0:K] = z_part
    parts[3].start()
    y_low = finish(y_part.T, 2, mcol > 0)
    z_lower = finish(z_part.T, 4, mrow > 0)

    def start_border():
        parts[2].wait()
        parts[3].wait()
        y_high = finish(part_recv[2, :, 0:K], 3, mcol < mcols - 1)
        z_high = finish(part_recv[3, :, 0:K], 5, mrow < mrows - 1)
        own_out[:, 2 * K : 8 * K] = jnp.concatenate(
            [y_high, z_high, x_low, y_low, z_lower, jnp.zeros((K, K), F32)], axis=1
        )

        @pl.when(head)
        def _():
            border[sub] = jnp.concatenate([y_high, z_high], axis=1)
            cross(border, border_recv_sem, 0).start()
            cross(border, border_recv_sem, 1).start()

    def eliminate(index, pivot):
        coupling = chain[index][:, K : 2 * K]
        unit = (iota((K, K), 0) == iota((K, K), 1)).astype(F32)
        state = jnp.concatenate([pivot, jnp.zeros((K, K), F32)], axis=1)
        extra = jnp.concatenate([coupling, unit], axis=1)
        state = [state[8 * n : 8 * n + 8] for n in range(8)]
        inverse = [extra[8 * n : 8 * n + 8] for n in range(8)]
        for now in range(8):
            columns = {
                n: [
                    jnp.broadcast_to(state[n][:, 8 * now + c : 8 * now + c + 1], (8, 128))
                    for c in range(8)
                ]
                for n in range(now, 8)
            }
            lower = {}
            scale = []
            for c in range(8):
                value = columns[now][c][c : c + 1]
                for k in range(c):
                    value = value - lower[c, k] * lower[c, k]
                scale.append(lax.rsqrt(value))
                for r in range(c + 1, 8):
                    value = columns[now][c][r : r + 1]
                    for k in range(c):
                        value = value - lower[r, k] * lower[c, k]
                    lower[r, c] = value * scale[c]
            lines, lines_inverse = [], []
            for c in range(8):
                line_now = state[now][c : c + 1]
                line_inverse = inverse[now][c : c + 1]
                for k in range(c):
                    line_now = line_now - lower[c, k] * lines[k]
                    line_inverse = line_inverse - lower[c, k] * lines_inverse[k]
                lines.append(line_now * scale[c])
                lines_inverse.append(line_inverse * scale[c])
                at = 8 * now + c
                pivots[index, at : at + 1, :] = lines[c]
                solver[index, at : at + 1, :] = lines_inverse[c]
            for n in range(now + 1, 8):
                factors = []
                for c in range(8):
                    factor = columns[n][c]
                    for k in range(c):
                        factor = factor - factors[k] * lower[c, k]
                    factors.append(factor * scale[c])
                for c in range(8):
                    state[n] = state[n] - factors[c] * lines[c]
                    inverse[n] = inverse[n] - factors[c] * lines_inverse[c]

    def arrive(buffer, recv, slot):
        @pl.when(sub != slot)
        def _():
            landed(buffer, recv, slot).wait_recv()

    def result(index, which):
        return remote(
            solver.at[index],
            solver.at[index],
            solver_send_sem.at[index, which],
            solver_recv_sem.at[index],
            ({"mcol": j_next}, {"mrow": i_next})[which],
        )

    def factor(index, pivot):
        following = jnp.minimum(index + 1, SUB - 1)

        @pl.when(index < SUB - 1)
        def _():
            arrive(chain, chain_recv_sem, following)

        eliminate(index, pivot)
        result(index, 0).start()
        result(index, 1).start()
        coupled = solver[index, :, 0:K]
        return chain[following][:, 0:K] - dot_tn(coupled, coupled, HI)

    lane = iota((K, 8 * K), 1) >> 6

    def placed(index):
        values = border[index]
        first = jnp.concatenate([values[:, 0:K]] * 8, axis=1)
        other = jnp.concatenate([values[:, K : 2 * K]] * 8, axis=1)
        first = jnp.where(lane == index, first, 0.0)
        other = jnp.where(lane == index, other, 0.0)
        return jnp.concatenate([first, other], axis=1)

    def solve(index, carry):
        result(index, 0).wait_recv()
        values = solver[index]
        solved = dot_nn(values[:, K : 2 * K], xin[...], HI)
        xall[pl.ds(pl.multiple_of(index * K, K), K), :] = solved
        following = placed(jnp.minimum(index + 1, SUB - 1))
        xin[...] = following - dot_tn(values[:, 0:K], solved, HI)
        return carry

    @pl.when(head)
    def _():
        arrive(chain, chain_recv_sem, 0)
        pivot = lax.fori_loop(0, 1, factor, chain[0][:, 0:K])
        start_border()
        lax.fori_loop(1, SUB, factor, pivot)

    @pl.when(jnp.logical_not(head))
    def _():
        start_border()

    @pl.when(head)
    def _():
        upper = iota((K, K), 0) <= iota((K, K), 1)
        factor_out[:, 0:K] = jnp.where(upper, pivots[sub, :, 0:K], 0.0).T
        factor_out[:, K : 2 * K] = solver[jnp.maximum(sub - 1, 0), :, 0:K].T
        for step in range(1, SUB):
            line(chain, chain_send_sem, chain_recv_sem, step).wait_send()
        for which in range(2):
            cross(border, border_recv_sem, which).wait_send()
            for index in range(SUB):
                result(index, which).wait_send()

    @pl.when(second | third)
    def _():
        landed(border, border_recv_sem, sub).wait_recv()
        for step in range(1, SUB):
            line(border, border_send_sem, border_recv_sem, step).start()
        for slot in range(SUB):
            arrive(border, border_recv_sem, slot)
        xin[...] = placed(0)
        lax.fori_loop(0, SUB, solve, 0)
        which = jnp.where(third, SUB, 0) + sub
        mine = xall[:, pl.ds(pl.multiple_of((which // 2) * 128, 128), 128)]
        mine = jnp.where(lax.rem(sub, 2) == 1, pltpu.roll(mine, K, 1), mine)
        factor_out[...] = mine.T[0:K, :]
        product_out[...] = dot_tn(mine, xall[...], HI)[0:K]
        for step in range(1, SUB):
            line(border, border_send_sem, border_recv_sem, step).wait_send()


def place_kernel(own_hbm, factors_hbm, product_hbm, out, own, factors, product, sems):
    copies = [
        pltpu.make_async_copy(source, target, sems.at[n])
        for n, (source, target) in enumerate(
            ((own_hbm, own), (factors_hbm, factors), (product_hbm, product))
        )
    ]
    for copy in copies:
        copy.start()
    mrow = lax.axis_index("mrow")
    mcol = lax.axis_index("mcol")
    sub = lax.axis_index("sub")
    mrows = lax.axis_size("mrow")
    mcols = lax.axis_size("mcol")
    position = (mrow * mcols + mcol) * SUB + sub
    head = (mrow == 0) & (mcol == 0)
    second = (mrow == 0) & (mcol == 1)
    third = (mrow == 1) & (mcol == 0)
    odd = lax.rem(sub, 2) == 1

    out[...] = jnp.zeros_like(out)
    for copy in copies:
        copy.wait()

    def tile(index):
        return pl.ds(pl.multiple_of(index * 128, 128), 128)

    def block(index):
        return own[:, index * K : (index + 1) * K]

    empty = jnp.zeros((K, K), F32)

    @pl.when(jnp.logical_not(head))
    def _():
        diagonal, x_high, y_high, z_high, x_low, y_low, z_low = (block(n) for n in range(7))
        here = position // 2
        pair_even = jnp.concatenate([diagonal, x_high], axis=1)
        pair_odd = jnp.concatenate([x_low, diagonal], axis=1)
        out[:, tile(here)] = jnp.where(odd, pair_odd, pair_even)

        @pl.when(odd & (sub < SUB - 1))
        def _():
            out[:, tile(here + 1)] = jnp.concatenate([x_high, empty], axis=1)

        @pl.when(jnp.logical_not(odd) & (sub > 0))
        def _():
            out[:, tile(here - 1)] = jnp.concatenate([empty, x_low], axis=1)

        def either(value):
            return jnp.where(
                odd,
                jnp.concatenate([empty, value], axis=1),
                jnp.concatenate([value, empty], axis=1),
            )

        for value, present, stride in (
            (y_high, mcol < mcols - 1, SUB // 2),
            (y_low, (mcol > 0) & jnp.logical_not(second), -(SUB // 2)),
            (z_high, mrow < mrows - 1, mcols * SUB // 2),
            (z_low, (mrow > 0) & jnp.logical_not(third), -(mcols * SUB // 2)),
        ):

            @pl.when(present)
            def _():
                out[:, tile(here + stride)] = either(value)

    @pl.when(head)
    def _():
        mine = factors[:, 0:K]
        before = factors[:, K : 2 * K]
        here = sub // 2
        out[:, tile(here)] = jnp.where(
            odd,
            jnp.concatenate([before, mine], axis=1),
            jnp.concatenate([mine, empty], axis=1),
        )

        @pl.when(jnp.logical_not(odd) & (sub > 0))
        def _():
            out[:, tile(here - 1)] = jnp.concatenate([empty, before], axis=1)

    @pl.when(second | third)
    def _():
        out[:, 0 : 8 * K] = factors[...]
        out[:, 8 * K : 16 * K] -= product[:, 0 : 8 * K]
        far = mcols * SUB * K
        out[:, far : far + 8 * K] -= product[:, 8 * K : 16 * K]


def shards(deflation, reaction, vector_counts):
    vmem = pl.BlockSpec(memory_space=pltpu.VMEM)
    results = pl.pallas_call(
        assemble_kernel,
        out_shape=(
            jax.ShapeDtypeStruct((K, 8 * K), F32),
            jax.ShapeDtypeStruct((K, 8 * K), F32),
            jax.ShapeDtypeStruct((K, 16 * K), F32),
        ),
        in_specs=[
            pl.BlockSpec(memory_space=pl.ANY),
            vmem,
            pl.BlockSpec(memory_space=pltpu.SMEM),
        ],
        out_specs=(vmem, vmem, vmem),
        scratch_shapes=[
            pltpu.VMEM((CX + 1, K, CY, CZ), BF16),
            pltpu.VMEM((ROWS + 16, 8 * CZ), BF16),
            pltpu.VMEM((ROWS, 8 * CZ), BF16),
            pltpu.VMEM((ROWS, ROWS), F32),
            pltpu.VMEM((CX, CY, CZ), F32),
            pltpu.VMEM((CX, 16, ROWS), F32),
            pltpu.VMEM((2, K, CZ), F32),
            pltpu.VMEM((CX, K, CZ), BF16),
            pltpu.VMEM((CX, K, CZ), BF16),
            pltpu.VMEM((CX, K, CZ), BF16),
            pltpu.VMEM((CX, 8, ROWS), F32),
            pltpu.VMEM((K, CY // 2, CZ), BF16),
            pltpu.VMEM((K, CY // 2, CZ), BF16),
            pltpu.VMEM((8, 128), F32),
            pltpu.VMEM((6, 8, 128), F32),
            pltpu.VMEM((4, K, 128), F32),
            pltpu.VMEM((4, K, 128), F32),
            pltpu.VMEM((SUB, K, 2 * K), F32),
            pltpu.VMEM((SUB, K, 2 * K), F32),
            pltpu.VMEM((SUB, K, 128), F32),
            pltpu.VMEM((SUB, K, 2 * K), F32),
            pltpu.VMEM((K, 16 * K), F32),
            pltpu.VMEM((SUB * K, 16 * K), F32),
            pltpu.SemaphoreType.DMA((CX,)),
            pltpu.SemaphoreType.DMA((6,)),
            pltpu.SemaphoreType.DMA((6,)),
            pltpu.SemaphoreType.DMA((2,)),
            pltpu.SemaphoreType.DMA((2,)),
            pltpu.SemaphoreType.DMA((CX,)),
            pltpu.SemaphoreType.DMA((CX,)),
            pltpu.SemaphoreType.DMA((CX,)),
            pltpu.SemaphoreType.DMA((CX,)),
            pltpu.SemaphoreType.DMA((4,)),
            pltpu.SemaphoreType.DMA((4,)),
            pltpu.SemaphoreType.DMA((SUB,)),
            pltpu.SemaphoreType.DMA((SUB,)),
            pltpu.SemaphoreType.DMA((SUB,)),
            pltpu.SemaphoreType.DMA((SUB,)),
            pltpu.SemaphoreType.DMA((2,)),
            pltpu.SemaphoreType.DMA((SUB, 2)),
            pltpu.SemaphoreType.DMA((SUB,)),
        ],
        compiler_params=pltpu.CompilerParams(
            collective_id=0, has_side_effects=True, vmem_limit_bytes=56 * 1024 * 1024
        ),
        name="assemble",
    )(deflation, reaction, vector_counts)
    return pl.pallas_call(
        place_kernel,
        out_shape=jax.ShapeDtypeStruct((K, 128 * K), F32),
        in_specs=[pl.BlockSpec(memory_space=pl.ANY)] * 3,
        out_specs=vmem,
        scratch_shapes=[
            pltpu.VMEM((K, 8 * K), F32),
            pltpu.VMEM((K, 8 * K), F32),
            pltpu.VMEM((K, 16 * K), F32),
            pltpu.SemaphoreType.DMA((3,)),
        ],
        compiler_params=pltpu.CompilerParams(vmem_limit_bytes=56 * 1024 * 1024),
        name="place",
    )(*results)


def solution(mesh):
    return jax.shard_map(
        shards,
        mesh=mesh,
        in_specs=(
            P(None, "sub", "mcol", "mrow"),
            P("sub", "mcol", "mrow"),
            P(("mrow", "mcol", "sub")),
        ),
        out_specs=P(("mrow", "mcol", "sub"), None),
        check_vma=False,
    )
```

```python
import functools

import jax
import jax.numpy as jnp
from jax import lax
from jax.experimental import pallas as pl
from jax.experimental.pallas import tpu as pltpu
from jax.sharding import PartitionSpec as P

MESH = pl.DeviceIdType.MESH
F32 = jnp.float32
BF16 = jnp.bfloat16
HI = lax.Precision.HIGHEST
K = 64
CX = 8
CY = 64
CZ = 256
ROWS = K * 8
SUB = 8
EARLY = 6


def dot_nt(a, b, precision=None):
    return lax.dot_general(
        a, b, (((1,), (1,)), ((), ())), precision=precision, preferred_element_type=F32
    )


def dot_nn(a, b, precision=None):
    return lax.dot_general(
        a, b, (((1,), (0,)), ((), ())), precision=precision, preferred_element_type=F32
    )


def dot_tn(a, b, precision=None):
    return lax.dot_general(
        a, b, (((0,), (0,)), ((), ())), precision=precision, preferred_element_type=F32
    )


def halves(value):
    high = value.astype(BF16)
    return high, (value - high.astype(F32)).astype(BF16)


def triple(dot, a, b):
    a_high, a_low = halves(a)
    b_high, b_low = halves(b)
    return dot(a_high, b_high) + (dot(a_high, b_low) + dot(a_low, b_high))


def iota(shape, axis):
    return lax.broadcasted_iota(jnp.int32, shape, axis)


def fold(product):
    same = (iota(product.shape, 0) & 7) == (iota(product.shape, 1) & 7)
    kept = jnp.where(same, product, 0.0).reshape(K, 8, ROWS).sum(axis=1)
    collect = ((iota((ROWS, K), 0) >> 3) == iota((ROWS, K), 1)).astype(F32)
    return dot_nn(kept, collect, HI)


def assemble_kernel(
    defl,
    react,
    count,
    own_out,
    factor_out,
    product_out,
    mbuf,
    left,
    right,
    acc,
    weight,
    zrows,
    yedge,
    ylow,
    yhigh,
    yrecv,
    zrecv,
    xrecv_low,
    xrecv_high,
    mask_own,
    mask_recv,
    part_send,
    part_recv,
    chain,
    border,
    pivots,
    solver,
    spread,
    xin,
    xall,
    load_sem,
    mask_send_sem,
    mask_recv_sem,
    face_send_sem,
    face_recv_sem,
    y_send_sem,
    y_recv_sem,
    z_send_sem,
    z_recv_sem,
    part_send_sem,
    part_recv_sem,
    chain_send_sem,
    chain_recv_sem,
    border_send_sem,
    border_recv_sem,
    cross_send_sem,
    solver_send_sem,
    solver_recv_sem,
):
    mrow = lax.axis_index("mrow")
    mcol = lax.axis_index("mcol")
    sub = lax.axis_index("sub")
    mrows = lax.axis_size("mrow")
    mcols = lax.axis_size("mcol")
    s_next, s_prev = lax.rem(sub + 1, SUB), lax.rem(sub + SUB - 1, SUB)
    j_next, j_prev = lax.rem(mcol + 1, mcols), lax.rem(mcol + mcols - 1, mcols)
    i_next, i_prev = lax.rem(mrow + 1, mrows), lax.rem(mrow + mrows - 1, mrows)
    head = (mrow == 0) & (mcol == 0)
    second = (mrow == 0) & (mcol == 1)
    third = (mrow == 1) & (mcol == 0)

    loads = [
        pltpu.make_async_copy(defl.at[:, x], mbuf.at[x], load_sem.at[x]) for x in range(CX)
    ]
    for load in loads:
        load.start()

    barrier = pltpu.get_barrier_semaphore()
    for step in range(1, SUB):
        pl.semaphore_signal(
            barrier,
            inc=1,
            device_id={"sub": lax.rem(sub + step, SUB)},
            device_id_type=MESH,
        )
    for axis, other in (
        ("mcol", j_next),
        ("mcol", j_prev),
        ("mrow", i_next),
        ("mrow", i_prev),
    ):
        pl.semaphore_signal(barrier, inc=1, device_id={axis: other}, device_id_type=MESH)

    live = count[0]
    mask_own[...] = (iota((8, 128), 1) < live).astype(F32)
    weight[...] = 3.0 + 0.5 * react[...]
    mbuf[CX] = jnp.zeros((K, CY, CZ), BF16)
    acc[...] = jnp.zeros_like(acc)
    part_send[...] = jnp.zeros_like(part_send)
    tail = iota((16, 8 * CZ), 0)
    spot = (tail & 7) * CZ + (tail >> 3) * (CZ - 1)
    left[ROWS : ROWS + 16, :] = (iota((16, 8 * CZ), 1) == spot).astype(F32).astype(BF16)

    def remote(src, dst, send, recv, target):
        return pltpu.make_async_remote_copy(
            src_ref=src,
            dst_ref=dst,
            send_sem=send,
            recv_sem=recv,
            device_id=target,
            device_id_type=MESH,
        )

    xface_up = remote(
        defl.at[:, CX - 1, 0 : CY // 2],
        xrecv_low,
        face_send_sem.at[0],
        face_recv_sem.at[0],
        {"sub": s_next},
    )
    xface_down = remote(
        defl.at[:, 0, CY // 2 : CY],
        xrecv_high,
        face_send_sem.at[1],
        face_recv_sem.at[1],
        {"sub": s_prev},
    )
    group = 4
    last_lane = iota((1, 1, 128), 2) == 127
    last_row = iota((1, 8, 1), 1) == 7

    def flat(value):
        return value.reshape(8 * group, CZ).astype(BF16)

    def stage_group(x, first, row):
        here = mbuf[x, pl.ds(first, group)].astype(F32)
        after_x = mbuf[x + 1, pl.ds(first, group)].astype(F32)
        turned_low = pltpu.roll(here[:, :, 0:128], 127, 2)
        turned_high = pltpu.roll(here[:, :, 128:256], 127, 2)
        after_z = jnp.concatenate(
            [
                jnp.where(last_lane, turned_high, turned_low),
                jnp.where(last_lane, 0.0, turned_high),
            ],
            axis=2,
        )
        turned = [pltpu.roll(here[:, 8 * n : 8 * n + 8, :], 7, 1) for n in range(8)]
        turned.append(jnp.zeros((group, 8, CZ), F32))
        place = pl.ds(row, 8 * group)
        for block in range(8):
            part = slice(8 * block, 8 * block + 8)
            lanes = slice(block * CZ, (block + 1) * CZ)
            after_y = jnp.where(last_row, turned[block + 1], turned[block])
            half = weight[x, part][None] * here[:, part] - after_x[:, part]
            half = half - after_y - after_z[:, part]
            left[place, lanes] = flat(half)
            right[place, lanes] = flat(here[:, part])
        for n in range(group):
            yedge[0, pl.ds(first + n, 1), :] = here[n, 0:1, :]
            yedge[1, pl.ds(first + n, 1), :] = here[n, CY - 1 : CY, :]

    def y_face(x):
        return remote(
            yhigh.at[x], yrecv.at[x], y_send_sem.at[x], y_recv_sem.at[x], {"mcol": j_next}
        )

    def z_face(x):
        return remote(
            zrows.at[x, pl.ds(8, 8)],
            zrecv.at[x],
            z_send_sem.at[x],
            z_recv_sem.at[x],
            {"mrow": i_next},
        )

    y_up, y_down = mcol < mcols - 1, mcol > 0
    z_up, z_down = mrow < mrows - 1, mrow > 0

    def start_faces(x):
        @pl.when(y_up)
        def _():
            y_face(x).start()

        @pl.when(z_up)
        def _():
            z_face(x).start()

    def silent_plane(x, carry):
        @pl.when(x < EARLY)
        def _():
            pltpu.make_async_copy(
                defl.at[:, x + 1], mbuf.at[x + 1], load_sem.at[x + 1]
            ).wait()

        def part(step, inner):
            for q in range(K // 2 // group):
                first = pl.multiple_of(step * (K // 2) + q * group, group)
                row = pl.multiple_of(step * (K // 2 * 8) + q * group * 8, group * 8)
                stage_group(x, first, row)
            return inner

        lax.fori_loop(0, 2, part, 0)
        ylow[x] = yedge[0].astype(BF16)
        yhigh[x] = yedge[1].astype(BF16)
        product = dot_nt(left[...], right[...])
        acc[...] += product[:ROWS]
        zrows[x] = product[ROWS : ROWS + 16]
        return carry

    def plane(x, carry):
        silent_plane(x, carry)
        start_faces(x)
        return carry

    loads[0].wait()
    lax.fori_loop(0, 1, silent_plane, 0)
    pl.semaphore_wait(barrier, SUB - 1 + 4)
    xface_up.start()
    xface_down.start()

    masks = []
    for slot, target in enumerate(
        (
            {"sub": s_next},
            {"sub": s_prev},
            {"mcol": j_next},
            {"mcol": j_prev},
            {"mrow": i_next},
            {"mrow": i_prev},
        )
    ):
        masks.append(
            remote(
                mask_own,
                mask_recv.at[slot],
                mask_send_sem.at[slot],
                mask_recv_sem.at[slot],
                target,
            )
        )
        masks[-1].start()
    start_faces(0)
    lax.fori_loop(1, EARLY, plane, 0)

    for load in loads[EARLY + 1 :]:
        load.wait()
    xface_up.wait()
    xface_down.wait()

    def stage(step, inner):
        for q in range(2):
            first = pl.multiple_of(8 * step + q * group, group)
            place = pl.ds(pl.multiple_of(64 * step + q * group * 8, group * 8), group * 8)
            chosen = pl.ds(first, group)
            sources = (
                (mbuf[0, chosen, 0 : CY // 2, :], xrecv_low[chosen]),
                (last_half[chosen], xrecv_high[chosen]),
            )
            for which, (mine, theirs) in enumerate(sources):
                mine = mine.astype(F32)
                theirs = theirs.astype(F32)
                for block in range(4):
                    part = slice(8 * block, 8 * block + 8)
                    lanes = slice((4 * which + block) * CZ, (4 * which + block + 1) * CZ)
                    right[place, lanes] = flat(mine[:, part])
                    left[place, lanes] = flat(theirs[:, part])
        return inner

    last_half = mbuf.at[CX - 1, :, CY // 2 : CY, :]
    lax.fori_loop(0, K // 8, stage, 0)
    low_part = fold(dot_nt(left[0:ROWS, 0 : 4 * CZ], right[:, 0 : 4 * CZ]))
    high_part = fold(dot_nt(right[:, 4 * CZ : 8 * CZ], left[0:ROWS, 4 * CZ : 8 * CZ]))
    part_send[0, :, 0:K] = low_part
    part_send[1, :, 0:K] = high_part.T
    parts = [
        remote(
            part_send.at[slot],
            part_recv.at[slot],
            part_send_sem.at[slot],
            part_recv_sem.at[slot],
            target,
        )
        for slot, target in enumerate(
            ({"sub": s_prev}, {"sub": s_next}, {"mcol": j_prev}, {"mrow": i_prev})
        )
    ]
    parts[0].start()
    parts[1].start()

    lax.fori_loop(EARLY, CX, plane, 0)

    own_row = (iota((K, K), 0) < live).astype(F32)
    own_col = mask_own[0:1, 0:K]
    diag = (iota((K, K), 0) == iota((K, K), 1)).astype(F32)

    def finish(block, slot, present):
        kept = own_row * mask_recv[slot, 0:1, 0:K]
        return -block * (kept * jnp.where(present, 1.0, 0.0))

    gram = fold(acc[...])
    diagonal = (gram + gram.T) * own_row * own_col + diag * (1.0 - own_row)
    for mask in masks:
        mask.wait()
    parts[0].wait()
    parts[1].wait()
    x_high = finish(high_part + part_recv[0, :, 0:K], 1, sub < SUB - 1)

    def cross(buffer, recv, which):
        return remote(
            buffer.at[sub],
            buffer.at[sub],
            cross_send_sem.at[which],
            recv.at[sub],
            ({"mcol": j_next}, {"mrow": i_next})[which],
        )

    def line(buffer, send, recv, step):
        return remote(
            buffer.at[sub],
            buffer.at[sub],
            send.at[step],
            recv.at[sub],
            {"sub": lax.rem(sub + step, SUB)},
        )

    def landed(buffer, recv, slot):
        return remote(
            buffer.at[slot],
            buffer.at[slot],
            cross_send_sem.at[0],
            recv.at[slot],
            {"mcol": j_next},
        )

    @pl.when(head)
    def _():
        chain[sub] = jnp.concatenate([diagonal, x_high], axis=1)
        for step in range(1, SUB):
            line(chain, chain_send_sem, chain_recv_sem, step).start()

    x_low = finish(low_part.T + part_recv[1, :, 0:K], 0, sub > 0)
    own_out[:, 0 : 2 * K] = jnp.concatenate([diagonal, x_high], axis=1)
    own_out[:, 4 * K : 5 * K] = x_low

    @pl.when(y_down)
    def _():
        for x in range(CX):
            y_face(x).wait_recv()
        y_part = dot_nt(
            jnp.concatenate([yrecv[x] for x in range(CX)], axis=1),
            jnp.concatenate([ylow[x] for x in range(CX)], axis=1),
        )
        part_send[2, :, 0:K] = y_part
        parts[2].start()
        own_out[:, 5 * K : 6 * K] = finish(y_part.T, 2, True)

    @pl.when(z_down)
    def _():
        for x in range(CX):
            z_face(x).wait_recv()
        z_low = zrows[:, 0:8, :].reshape(K, ROWS)
        z_part = fold(dot_tn(zrecv[...].reshape(K, ROWS), z_low))
        part_send[3, :, 0:K] = z_part
        parts[3].start()
        own_out[:, 6 * K : 7 * K] = finish(z_part.T, 4, True)

    def start_border():
        for up, down, part, face in (
            (y_up, y_down, parts[2], y_face),
            (z_up, z_down, parts[3], z_face),
        ):

            @pl.when(up)
            def _():
                part.wait_recv()
                for x in range(CX):
                    face(x).wait_send()

            @pl.when(down)
            def _():
                part.wait_send()

        y_high = finish(part_recv[2, :, 0:K], 3, y_up)
        z_high = finish(part_recv[3, :, 0:K], 5, z_up)
        own_out[:, 2 * K : 4 * K] = jnp.concatenate([y_high, z_high], axis=1)

        @pl.when(head)
        def _():
            border[sub] = jnp.concatenate([y_high, z_high], axis=1)
            cross(border, border_recv_sem, 0).start()
            cross(border, border_recv_sem, 1).start()

    def eliminate(index, pivot):
        coupling = chain[index][:, K : 2 * K]
        unit = (iota((K, K), 0) == iota((K, K), 1)).astype(F32)
        state = jnp.concatenate([pivot, jnp.zeros((K, K), F32)], axis=1)
        extra = jnp.concatenate([coupling, unit], axis=1)
        state = [state[8 * n : 8 * n + 8] for n in range(8)]
        inverse = [extra[8 * n : 8 * n + 8] for n in range(8)]
        for now in range(8):
            columns = {
                n: [
                    jnp.broadcast_to(state[n][:, 8 * now + c : 8 * now + c + 1], (8, 128))
                    for c in range(8)
                ]
                for n in range(now, 8)
            }
            for c in range(8):
                spread[now % 2, c] = columns[now][c]

            def entry(r, c):
                return jnp.broadcast_to(spread[now % 2, c, r : r + 1, :], (8, 128))

            lower = {}
            scale = []
            for c in range(8):
                value = entry(c, c)
                for k in range(c):
                    value = value - lower[c, k] * lower[c, k]
                scale.append(lax.rsqrt(value))
                for r in range(c + 1, 8):
                    value = entry(r, c)
                    for k in range(c):
                        value = value - lower[r, k] * lower[c, k]
                    lower[r, c] = value * scale[c]
            lines, lines_inverse = [], []
            for c in range(8):
                line_now = state[now][c : c + 1]
                line_inverse = inverse[now][c : c + 1]
                for k in range(c):
                    line_now = line_now - lower[c, k] * lines[k]
                    line_inverse = line_inverse - lower[c, k] * lines_inverse[k]
                lines.append(line_now * scale[c])
                lines_inverse.append(line_inverse * scale[c])
                at = 8 * now + c
                pivots[index, at : at + 1, :] = lines[c][0:1]
                solver[index, at : at + 1, :] = lines_inverse[c][0:1]
            for n in range(now + 1, 8):
                factors = []
                for c in range(8):
                    factor = columns[n][c]
                    for k in range(c):
                        factor = factor - factors[k] * lower[c, k]
                    factors.append(factor * scale[c])
                for c in range(8):
                    state[n] = state[n] - factors[c] * lines[c]
                    inverse[n] = inverse[n] - factors[c] * lines_inverse[c]

    def arrive(buffer, recv, slot):
        @pl.when(sub != slot)
        def _():
            landed(buffer, recv, slot).wait_recv()

    def result(index, which):
        return remote(
            solver.at[index],
            solver.at[index],
            solver_send_sem.at[index, which],
            solver_recv_sem.at[index],
            ({"mcol": j_next}, {"mrow": i_next})[which],
        )

    def factor(index, pivot):
        following = jnp.minimum(index + 1, SUB - 1)

        @pl.when(index < SUB - 1)
        def _():
            arrive(chain, chain_recv_sem, following)

        eliminate(index, pivot)
        result(index, 0).start()
        result(index, 1).start()
        coupled = solver[index, :, 0:K]
        return chain[following][:, 0:K] - triple(dot_tn, coupled, coupled)

    lane = iota((K, 8 * K), 1) >> 6

    def placed(index):
        values = border[index]
        first = jnp.concatenate([values[:, 0:K]] * 8, axis=1)
        other = jnp.concatenate([values[:, K : 2 * K]] * 8, axis=1)
        first = jnp.where(lane == index, first, 0.0)
        other = jnp.where(lane == index, other, 0.0)
        return jnp.concatenate([first, other], axis=1)

    own_slot = jnp.where(third, SUB, 0) + sub
    own_tile = pl.ds(pl.multiple_of((own_slot // 2) * 128, 128), 128)

    def solve(index, carry):
        result(index, 0).wait_recv()
        values = solver[index]
        solved = triple(dot_nn, values[:, K : 2 * K], xin[...])
        xall[pl.ds(pl.multiple_of(index * K, K), K), :] = solved

        @pl.when(index < SUB - 1)
        def _():
            following = placed(jnp.minimum(index + 1, SUB - 1))
            xin[...] = following - triple(dot_tn, values[:, 0:K], solved)

        return carry

    @pl.when(head)
    def _():
        arrive(chain, chain_recv_sem, 0)
        pivot = lax.fori_loop(0, 1, factor, chain[0][:, 0:K])
        start_border()
        lax.fori_loop(1, SUB, factor, pivot)

    @pl.when(jnp.logical_not(head))
    def _():
        start_border()

    @pl.when(head)
    def _():
        upper = iota((K, K), 0) <= iota((K, K), 1)
        factor_out[:, 0:K] = jnp.where(upper, pivots[sub, :, 0:K], 0.0).T
        factor_out[:, K : 2 * K] = solver[jnp.maximum(sub - 1, 0), :, 0:K].T
        for step in range(1, SUB):
            line(chain, chain_send_sem, chain_recv_sem, step).wait_send()
        for which in range(2):
            cross(border, border_recv_sem, which).wait_send()
            for index in range(SUB):
                result(index, which).wait_send()

    @pl.when(second | third)
    def _():
        landed(border, border_recv_sem, sub).wait_recv()
        for step in range(1, SUB):
            line(border, border_send_sem, border_recv_sem, step).start()
        for slot in range(SUB):
            arrive(border, border_recv_sem, slot)
        xin[...] = placed(0)
        lax.fori_loop(0, SUB, solve, 0)
        odd = lax.rem(sub, 2) == 1
        mine = xall[:, own_tile]
        turned = mine.T
        factor_out[...] = jnp.where(odd, turned[K:], turned[0:K])
        product = triple(dot_tn, mine, xall[...])
        product_out[...] = jnp.where(odd, product[K:], product[0:K])
        for step in range(1, SUB):
            line(border, border_send_sem, border_recv_sem, step).wait_send()


def place_kernel(own_hbm, factors_hbm, product_hbm, out, own, factors, product, sems):
    copies = [
        pltpu.make_async_copy(source, target, sems.at[n])
        for n, (source, target) in enumerate(
            ((own_hbm, own), (factors_hbm, factors), (product_hbm, product))
        )
    ]
    for copy in copies:
        copy.start()
    mrow = lax.axis_index("mrow")
    mcol = lax.axis_index("mcol")
    sub = lax.axis_index("sub")
    mrows = lax.axis_size("mrow")
    mcols = lax.axis_size("mcol")
    position = (mrow * mcols + mcol) * SUB + sub
    head = (mrow == 0) & (mcol == 0)
    second = (mrow == 0) & (mcol == 1)
    third = (mrow == 1) & (mcol == 0)
    odd = lax.rem(sub, 2) == 1

    out[...] = jnp.zeros_like(out)
    for copy in copies:
        copy.wait()

    def tile(index):
        return pl.ds(pl.multiple_of(index * 128, 128), 128)

    def block(index):
        return own[:, index * K : (index + 1) * K]

    empty = jnp.zeros((K, K), F32)

    @pl.when(jnp.logical_not(head))
    def _():
        diagonal, x_high, y_high, z_high, x_low, y_low, z_low = (block(n) for n in range(7))
        here = position // 2
        pair_even = jnp.concatenate([diagonal, x_high], axis=1)
        pair_odd = jnp.concatenate([x_low, diagonal], axis=1)
        out[:, tile(here)] = jnp.where(odd, pair_odd, pair_even)

        @pl.when(odd & (sub < SUB - 1))
        def _():
            out[:, tile(here + 1)] = jnp.concatenate([x_high, empty], axis=1)

        @pl.when(jnp.logical_not(odd) & (sub > 0))
        def _():
            out[:, tile(here - 1)] = jnp.concatenate([empty, x_low], axis=1)

        def either(value):
            return jnp.where(
                odd,
                jnp.concatenate([empty, value], axis=1),
                jnp.concatenate([value, empty], axis=1),
            )

        for value, present, stride in (
            (y_high, mcol < mcols - 1, SUB // 2),
            (y_low, (mcol > 0) & jnp.logical_not(second), -(SUB // 2)),
            (z_high, mrow < mrows - 1, mcols * SUB // 2),
            (z_low, (mrow > 0) & jnp.logical_not(third), -(mcols * SUB // 2)),
        ):

            @pl.when(present)
            def _():
                out[:, tile(here + stride)] = either(value)

    @pl.when(head)
    def _():
        mine = factors[:, 0:K]
        before = factors[:, K : 2 * K]
        here = sub // 2
        out[:, tile(here)] = jnp.where(
            odd,
            jnp.concatenate([before, mine], axis=1),
            jnp.concatenate([mine, empty], axis=1),
        )

        @pl.when(jnp.logical_not(odd) & (sub > 0))
        def _():
            out[:, tile(here - 1)] = jnp.concatenate([empty, before], axis=1)

    @pl.when(second | third)
    def _():
        out[:, 0 : 8 * K] = factors[...]
        out[:, 8 * K : 16 * K] -= product[:, 0 : 8 * K]
        far = mcols * SUB * K
        out[:, far : far + 8 * K] -= product[:, 8 * K : 16 * K]


def shards(deflation, reaction, vector_counts):
    vmem = pl.BlockSpec(memory_space=pltpu.VMEM)
    results = pl.pallas_call(
        assemble_kernel,
        out_shape=(
            jax.ShapeDtypeStruct((K, 8 * K), F32),
            jax.ShapeDtypeStruct((K, 8 * K), F32),
            jax.ShapeDtypeStruct((K, 16 * K), F32),
        ),
        in_specs=[
            pl.BlockSpec(memory_space=pl.ANY),
            vmem,
            pl.BlockSpec(memory_space=pltpu.SMEM),
        ],
        out_specs=(vmem, vmem, vmem),
        scratch_shapes=[
            pltpu.VMEM((CX + 1, K, CY, CZ), BF16),
            pltpu.VMEM((ROWS + 16, 8 * CZ), BF16),
            pltpu.VMEM((ROWS, 8 * CZ), BF16),
            pltpu.VMEM((ROWS, ROWS), F32),
            pltpu.VMEM((CX, CY, CZ), F32),
            pltpu.VMEM((CX, 16, ROWS), F32),
            pltpu.VMEM((2, K, CZ), F32),
            pltpu.VMEM((CX, K, CZ), BF16),
            pltpu.VMEM((CX, K, CZ), BF16),
            pltpu.VMEM((CX, K, CZ), BF16),
            pltpu.VMEM((CX, 8, ROWS), F32),
            pltpu.VMEM((K, CY // 2, CZ), BF16),
            pltpu.VMEM((K, CY // 2, CZ), BF16),
            pltpu.VMEM((8, 128), F32),
            pltpu.VMEM((6, 8, 128), F32),
            pltpu.VMEM((4, K, 128), F32),
            pltpu.VMEM((4, K, 128), F32),
            pltpu.VMEM((SUB, K, 2 * K), F32),
            pltpu.VMEM((SUB, K, 2 * K), F32),
            pltpu.VMEM((SUB, K, 128), F32),
            pltpu.VMEM((SUB, K, 2 * K), F32),
            pltpu.VMEM((2, 8, 8, 128), F32),
            pltpu.VMEM((K, 16 * K), F32),
            pltpu.VMEM((SUB * K, 16 * K), F32),
            pltpu.SemaphoreType.DMA((CX,)),
            pltpu.SemaphoreType.DMA((6,)),
            pltpu.SemaphoreType.DMA((6,)),
            pltpu.SemaphoreType.DMA((2,)),
            pltpu.SemaphoreType.DMA((2,)),
            pltpu.SemaphoreType.DMA((CX,)),
            pltpu.SemaphoreType.DMA((CX,)),
            pltpu.SemaphoreType.DMA((CX,)),
            pltpu.SemaphoreType.DMA((CX,)),
            pltpu.SemaphoreType.DMA((4,)),
            pltpu.SemaphoreType.DMA((4,)),
            pltpu.SemaphoreType.DMA((SUB,)),
            pltpu.SemaphoreType.DMA((SUB,)),
            pltpu.SemaphoreType.DMA((SUB,)),
            pltpu.SemaphoreType.DMA((SUB,)),
            pltpu.SemaphoreType.DMA((2,)),
            pltpu.SemaphoreType.DMA((SUB, 2)),
            pltpu.SemaphoreType.DMA((SUB,)),
        ],
        compiler_params=pltpu.CompilerParams(
            collective_id=0, has_side_effects=True, vmem_limit_bytes=56 * 1024 * 1024
        ),
        name="assemble",
    )(deflation, reaction, vector_counts)
    return pl.pallas_call(
        place_kernel,
        out_shape=jax.ShapeDtypeStruct((K, 128 * K), F32),
        in_specs=[pl.BlockSpec(memory_space=pl.ANY)] * 3,
        out_specs=vmem,
        scratch_shapes=[
            pltpu.VMEM((K, 8 * K), F32),
            pltpu.VMEM((K, 8 * K), F32),
            pltpu.VMEM((K, 16 * K), F32),
            pltpu.SemaphoreType.DMA((3,)),
        ],
        compiler_params=pltpu.CompilerParams(vmem_limit_bytes=56 * 1024 * 1024),
        name="place",
    )(*results)


def solution(mesh):
    return jax.shard_map(
        shards,
        mesh=mesh,
        in_specs=(
            P(None, "sub", "mcol", "mrow"),
            P("sub", "mcol", "mrow"),
            P(("mrow", "mcol", "sub")),
        ),
        out_specs=P(("mrow", "mcol", "sub"), None),
        check_vma=False,
    )
```

```python
import functools

import jax
import jax.numpy as jnp
from jax import lax
from jax.experimental import pallas as pl
from jax.experimental.pallas import tpu as pltpu
from jax.sharding import PartitionSpec as P

MESH = pl.DeviceIdType.MESH
F32 = jnp.float32
BF16 = jnp.bfloat16
HI = lax.Precision.HIGHEST
K = 64
CX = 8
CY = 64
CZ = 256
ROWS = K * 8
SUB = 8
EARLY = 6


def dot_nt(a, b, precision=None):
    return lax.dot_general(
        a, b, (((1,), (1,)), ((), ())), precision=precision, preferred_element_type=F32
    )


def dot_nn(a, b, precision=None):
    return lax.dot_general(
        a, b, (((1,), (0,)), ((), ())), precision=precision, preferred_element_type=F32
    )


def dot_tn(a, b, precision=None):
    return lax.dot_general(
        a, b, (((0,), (0,)), ((), ())), precision=precision, preferred_element_type=F32
    )


def halves(value):
    high = value.astype(BF16)
    return high, (value - high.astype(F32)).astype(BF16)


def triple(dot, a, b):
    a_high, a_low = halves(a)
    b_high, b_low = halves(b)
    return dot(a_high, b_high) + (dot(a_high, b_low) + dot(a_low, b_high))


def iota(shape, axis):
    return lax.broadcasted_iota(jnp.int32, shape, axis)


def fold(product):
    same = (iota(product.shape, 0) & 7) == (iota(product.shape, 1) & 7)
    kept = jnp.where(same, product, 0.0).reshape(K, 8, ROWS).sum(axis=1)
    collect = ((iota((ROWS, K), 0) >> 3) == iota((ROWS, K), 1)).astype(F32)
    collect = collect.astype(BF16)
    high, rest = kept.astype(BF16), kept - kept.astype(BF16).astype(F32)
    middle, low = halves(rest)
    return dot_nn(high, collect) + (dot_nn(middle, collect) + dot_nn(low, collect))


def assemble_kernel(
    defl,
    react,
    count,
    own_out,
    factor_out,
    product_out,
    mbuf,
    left,
    right,
    acc,
    weight,
    zrows,
    yedge,
    ylow,
    yhigh,
    yrecv,
    zrecv,
    xrecv_low,
    xrecv_high,
    mask_own,
    mask_recv,
    part_send,
    part_recv,
    chain,
    border,
    pivots,
    solver,
    spread,
    xin,
    xall,
    load_sem,
    field_sem,
    mask_send_sem,
    mask_recv_sem,
    face_send_sem,
    face_recv_sem,
    y_send_sem,
    y_recv_sem,
    z_send_sem,
    z_recv_sem,
    part_send_sem,
    part_recv_sem,
    chain_send_sem,
    chain_recv_sem,
    border_send_sem,
    border_recv_sem,
    cross_send_sem,
    solver_send_sem,
    solver_recv_sem,
):
    mrow = lax.axis_index("mrow")
    mcol = lax.axis_index("mcol")
    sub = lax.axis_index("sub")
    mrows = lax.axis_size("mrow")
    mcols = lax.axis_size("mcol")
    s_next, s_prev = lax.rem(sub + 1, SUB), lax.rem(sub + SUB - 1, SUB)
    j_next, j_prev = lax.rem(mcol + 1, mcols), lax.rem(mcol + mcols - 1, mcols)
    i_next, i_prev = lax.rem(mrow + 1, mrows), lax.rem(mrow + mrows - 1, mrows)
    head = (mrow == 0) & (mcol == 0)
    second = (mrow == 0) & (mcol == 1)
    third = (mrow == 1) & (mcol == 0)

    loads = [
        pltpu.make_async_copy(defl.at[:, x], mbuf.at[x], load_sem.at[x]) for x in range(CX)
    ]
    field = pltpu.make_async_copy(react, weight, field_sem)
    for load in loads[0:2]:
        load.start()
    field.start()
    loads[2].start()

    barrier = pltpu.get_barrier_semaphore()
    for step in range(1, SUB):
        pl.semaphore_signal(
            barrier,
            inc=1,
            device_id={"sub": lax.rem(sub + step, SUB)},
            device_id_type=MESH,
        )
    for axis, other in (
        ("mcol", j_next),
        ("mcol", j_prev),
        ("mrow", i_next),
        ("mrow", i_prev),
    ):
        pl.semaphore_signal(barrier, inc=1, device_id={axis: other}, device_id_type=MESH)

    live = count[0]
    mask_own[...] = (iota((8, 128), 1) < live).astype(F32)
    mbuf[CX] = jnp.zeros((K, CY, CZ), BF16)
    acc[...] = jnp.zeros_like(acc)
    part_send[...] = jnp.zeros_like(part_send)
    tail = iota((16, 8 * CZ), 0)
    spot = (tail & 7) * CZ + (tail >> 3) * (CZ - 1)
    left[ROWS : ROWS + 16, :] = (iota((16, 8 * CZ), 1) == spot).astype(F32).astype(BF16)

    def remote(src, dst, send, recv, target):
        return pltpu.make_async_remote_copy(
            src_ref=src,
            dst_ref=dst,
            send_sem=send,
            recv_sem=recv,
            device_id=target,
            device_id_type=MESH,
        )

    xface_up = remote(
        defl.at[:, CX - 1, 0 : CY // 2],
        xrecv_low,
        face_send_sem.at[0],
        face_recv_sem.at[0],
        {"sub": s_next},
    )
    xface_down = remote(
        defl.at[:, 0, CY // 2 : CY],
        xrecv_high,
        face_send_sem.at[1],
        face_recv_sem.at[1],
        {"sub": s_prev},
    )
    group = 4
    last_lane = iota((1, 1, 128), 2) == 127
    last_row = iota((1, 8, 1), 1) == 7

    def flat(value):
        return value.reshape(8 * group, CZ).astype(BF16)

    def stage_group(x, first, row):
        here = mbuf[x, pl.ds(first, group)].astype(F32)
        after_x = mbuf[x + 1, pl.ds(first, group)].astype(F32)
        turned_low = pltpu.roll(here[:, :, 0:128], 127, 2)
        turned_high = pltpu.roll(here[:, :, 128:256], 127, 2)
        after_z = jnp.concatenate(
            [
                jnp.where(last_lane, turned_high, turned_low),
                jnp.where(last_lane, 0.0, turned_high),
            ],
            axis=2,
        )
        turned = [pltpu.roll(here[:, 8 * n : 8 * n + 8, :], 7, 1) for n in range(8)]
        turned.append(jnp.zeros((group, 8, CZ), F32))
        place = pl.ds(row, 8 * group)
        for block in range(8):
            part = slice(8 * block, 8 * block + 8)
            lanes = slice(block * CZ, (block + 1) * CZ)
            after_y = jnp.where(last_row, turned[block + 1], turned[block])
            half = weight[x, part][None] * here[:, part] - after_x[:, part]
            half = half - after_y - after_z[:, part]
            left[place, lanes] = flat(half)
            right[place, lanes] = flat(here[:, part])
        for n in range(group):
            yedge[0, pl.ds(first + n, 1), :] = here[n, 0:1, :]
            yedge[1, pl.ds(first + n, 1), :] = here[n, CY - 1 : CY, :]

    def y_face(x):
        return remote(
            yhigh.at[x], yrecv.at[x], y_send_sem.at[x], y_recv_sem.at[x], {"mcol": j_next}
        )

    def z_face(x):
        return remote(
            zrows.at[x, pl.ds(8, 8)],
            zrecv.at[x],
            z_send_sem.at[x],
            z_recv_sem.at[x],
            {"mrow": i_next},
        )

    y_up, y_down = mcol < mcols - 1, mcol > 0
    z_up, z_down = mrow < mrows - 1, mrow > 0

    def start_faces(x):
        @pl.when(y_up)
        def _():
            y_face(x).start()

        @pl.when(z_up)
        def _():
            z_face(x).start()

    def silent_plane(x, carry):
        @pl.when(x + 3 < CX)
        def _():
            pltpu.make_async_copy(
                defl.at[:, x + 3], mbuf.at[x + 3], load_sem.at[x + 3]
            ).start()

        @pl.when(x < EARLY)
        def _():
            pltpu.make_async_copy(
                defl.at[:, x + 1], mbuf.at[x + 1], load_sem.at[x + 1]
            ).wait()

        def part(step, inner):
            for q in range(K // 2 // group):
                first = pl.multiple_of(step * (K // 2) + q * group, group)
                row = pl.multiple_of(step * (K // 2 * 8) + q * group * 8, group * 8)
                stage_group(x, first, row)
            return inner

        lax.fori_loop(0, 2, part, 0)
        ylow[x] = yedge[0].astype(BF16)
        yhigh[x] = yedge[1].astype(BF16)
        product = dot_nt(left[...], right[...])
        acc[...] += product[:ROWS]
        zrows[x] = product[ROWS : ROWS + 16]
        return carry

    def plane(x, carry):
        silent_plane(x, carry)
        start_faces(x)
        return carry

    field.wait()
    weight[...] = 3.0 + 0.5 * weight[...]
    loads[0].wait()
    lax.fori_loop(0, 1, silent_plane, 0)
    pl.semaphore_wait(barrier, SUB - 1 + 4)
    xface_up.start()
    xface_down.start()

    masks = []
    for slot, target in enumerate(
        (
            {"sub": s_next},
            {"sub": s_prev},
            {"mcol": j_next},
            {"mcol": j_prev},
            {"mrow": i_next},
            {"mrow": i_prev},
        )
    ):
        masks.append(
            remote(
                mask_own,
                mask_recv.at[slot],
                mask_send_sem.at[slot],
                mask_recv_sem.at[slot],
                target,
            )
        )
        masks[-1].start()
    start_faces(0)
    lax.fori_loop(1, EARLY, plane, 0)

    for load in loads[EARLY + 1 :]:
        load.wait()
    xface_up.wait()
    xface_down.wait()

    def stage(step, inner):
        for q in range(2):
            first = pl.multiple_of(8 * step + q * group, group)
            place = pl.ds(pl.multiple_of(64 * step + q * group * 8, group * 8), group * 8)
            chosen = pl.ds(first, group)
            sources = (
                (mbuf[0, chosen, 0 : CY // 2, :], xrecv_low[chosen]),
                (last_half[chosen], xrecv_high[chosen]),
            )
            for which, (mine, theirs) in enumerate(sources):
                mine = mine.astype(F32)
                theirs = theirs.astype(F32)
                for block in range(4):
                    part = slice(8 * block, 8 * block + 8)
                    lanes = slice((4 * which + block) * CZ, (4 * which + block + 1) * CZ)
                    right[place, lanes] = flat(mine[:, part])
                    left[place, lanes] = flat(theirs[:, part])
        return inner

    last_half = mbuf.at[CX - 1, :, CY // 2 : CY, :]
    lax.fori_loop(0, K // 8, stage, 0)
    low_part = fold(dot_nt(left[0:ROWS, 0 : 4 * CZ], right[:, 0 : 4 * CZ]))
    high_part = fold(dot_nt(right[:, 4 * CZ : 8 * CZ], left[0:ROWS, 4 * CZ : 8 * CZ]))
    part_send[0, :, 0:K] = low_part
    part_send[1, :, 0:K] = high_part.T
    parts = [
        remote(
            part_send.at[slot],
            part_recv.at[slot],
            part_send_sem.at[slot],
            part_recv_sem.at[slot],
            target,
        )
        for slot, target in enumerate(
            ({"sub": s_prev}, {"sub": s_next}, {"mcol": j_prev}, {"mrow": i_prev})
        )
    ]
    parts[0].start()
    parts[1].start()

    lax.fori_loop(EARLY, CX, plane, 0)

    own_row = (iota((K, K), 0) < live).astype(F32)
    own_col = mask_own[0:1, 0:K]
    diag = (iota((K, K), 0) == iota((K, K), 1)).astype(F32)

    def finish(block, slot, present):
        kept = own_row * mask_recv[slot, 0:1, 0:K]
        return -block * (kept * jnp.where(present, 1.0, 0.0))

    gram = fold(acc[...])
    diagonal = (gram + gram.T) * own_row * own_col + diag * (1.0 - own_row)
    for mask in masks:
        mask.wait()
    parts[0].wait()
    parts[1].wait()
    x_high = finish(high_part + part_recv[0, :, 0:K], 1, sub < SUB - 1)

    def cross(buffer, recv, which):
        return remote(
            buffer.at[sub],
            buffer.at[sub],
            cross_send_sem.at[which],
            recv.at[sub],
            ({"mcol": j_next}, {"mrow": i_next})[which],
        )

    def line(buffer, send, recv, step):
        return remote(
            buffer.at[sub],
            buffer.at[sub],
            send.at[step],
            recv.at[sub],
            {"sub": lax.rem(sub + step, SUB)},
        )

    def landed(buffer, recv, slot):
        return remote(
            buffer.at[slot],
            buffer.at[slot],
            cross_send_sem.at[0],
            recv.at[slot],
            {"mcol": j_next},
        )

    @pl.when(head)
    def _():
        chain[sub] = jnp.concatenate([diagonal, x_high], axis=1)
        for step in range(1, SUB):
            line(chain, chain_send_sem, chain_recv_sem, step).start()

    x_low = finish(low_part.T + part_recv[1, :, 0:K], 0, sub > 0)
    own_out[:, 0 : 2 * K] = jnp.concatenate([diagonal, x_high], axis=1)
    own_out[:, 4 * K : 5 * K] = x_low

    @pl.when(y_down)
    def _():
        for x in range(CX):
            y_face(x).wait_recv()
        y_part = dot_nt(
            jnp.concatenate([yrecv[x] for x in range(CX)], axis=1),
            jnp.concatenate([ylow[x] for x in range(CX)], axis=1),
        )
        part_send[2, :, 0:K] = y_part
        parts[2].start()
        own_out[:, 5 * K : 6 * K] = finish(y_part.T, 2, True)

    @pl.when(z_down)
    def _():
        for x in range(CX):
            z_face(x).wait_recv()
        z_low = zrows[:, 0:8, :].reshape(K, ROWS)
        z_part = fold(dot_tn(zrecv[...].reshape(K, ROWS), z_low))
        part_send[3, :, 0:K] = z_part
        parts[3].start()
        own_out[:, 6 * K : 7 * K] = finish(z_part.T, 4, True)

    def start_border():
        for up, down, part, face in (
            (y_up, y_down, parts[2], y_face),
            (z_up, z_down, parts[3], z_face),
        ):

            @pl.when(up)
            def _():
                part.wait_recv()
                for x in range(CX):
                    face(x).wait_send()

            @pl.when(down)
            def _():
                part.wait_send()

        y_high = finish(part_recv[2, :, 0:K], 3, y_up)
        z_high = finish(part_recv[3, :, 0:K], 5, z_up)
        own_out[:, 2 * K : 4 * K] = jnp.concatenate([y_high, z_high], axis=1)

        @pl.when(head)
        def _():
            border[sub] = jnp.concatenate([y_high, z_high], axis=1)
            cross(border, border_recv_sem, 0).start()
            cross(border, border_recv_sem, 1).start()

    def eliminate(index, pivot):
        coupling = chain[index][:, K : 2 * K]
        unit = (iota((K, K), 0) == iota((K, K), 1)).astype(F32)
        state = jnp.concatenate([pivot, jnp.zeros((K, K), F32)], axis=1)
        extra = jnp.concatenate([coupling, unit], axis=1)
        state = [state[8 * n : 8 * n + 8] for n in range(8)]
        inverse = [extra[8 * n : 8 * n + 8] for n in range(8)]
        for now in range(8):
            columns = {
                n: [
                    jnp.broadcast_to(state[n][:, 8 * now + c : 8 * now + c + 1], (8, 128))
                    for c in range(8)
                ]
                for n in range(now, 8)
            }
            for c in range(8):
                spread[now % 2, c] = columns[now][c]

            def entry(r, c):
                return jnp.broadcast_to(spread[now % 2, c, r : r + 1, :], (8, 128))

            lower = {}
            scale = []
            for c in range(8):
                value = entry(c, c)
                for k in range(c):
                    value = value - lower[c, k] * lower[c, k]
                scale.append(lax.rsqrt(value))
                for r in range(c + 1, 8):
                    value = entry(r, c)
                    for k in range(c):
                        value = value - lower[r, k] * lower[c, k]
                    lower[r, c] = value * scale[c]
            lines, lines_inverse = [], []
            for c in range(8):
                line_now = state[now][c : c + 1]
                line_inverse = inverse[now][c : c + 1]
                for k in range(c):
                    line_now = line_now - lower[c, k] * lines[k]
                    line_inverse = line_inverse - lower[c, k] * lines_inverse[k]
                lines.append(line_now * scale[c])
                lines_inverse.append(line_inverse * scale[c])
                at = 8 * now + c
                pivots[index, at : at + 1, :] = lines[c][0:1]
                solver[index, at : at + 1, :] = lines_inverse[c][0:1]
            for n in range(now + 1, 8):
                factors = []
                for c in range(8):
                    factor = columns[n][c]
                    for k in range(c):
                        factor = factor - factors[k] * lower[c, k]
                    factors.append(factor * scale[c])
                for c in range(8):
                    state[n] = state[n] - factors[c] * lines[c]
                    inverse[n] = inverse[n] - factors[c] * lines_inverse[c]

    def arrive(buffer, recv, slot):
        @pl.when(sub != slot)
        def _():
            landed(buffer, recv, slot).wait_recv()

    def result(index, which):
        return remote(
            solver.at[index],
            solver.at[index],
            solver_send_sem.at[index, which],
            solver_recv_sem.at[index],
            ({"mcol": j_next}, {"mrow": i_next})[which],
        )

    def factor(index, pivot):
        following = jnp.minimum(index + 1, SUB - 1)

        @pl.when(index < SUB - 1)
        def _():
            arrive(chain, chain_recv_sem, following)

        eliminate(index, pivot)
        result(index, 0).start()
        result(index, 1).start()
        coupled = solver[index, :, 0:K]
        return chain[following][:, 0:K] - dot_tn(coupled, coupled, HI)

    lane = iota((K, 8 * K), 1) >> 6

    def placed(index):
        values = border[index]
        first = jnp.concatenate([values[:, 0:K]] * 8, axis=1)
        other = jnp.concatenate([values[:, K : 2 * K]] * 8, axis=1)
        first = jnp.where(lane == index, first, 0.0)
        other = jnp.where(lane == index, other, 0.0)
        return jnp.concatenate([first, other], axis=1)

    own_slot = jnp.where(third, SUB, 0) + sub
    own_tile = pl.ds(pl.multiple_of((own_slot // 2) * 128, 128), 128)

    def solve(index, carry):
        result(index, 0).wait_recv()
        values = solver[index]
        solved = triple(dot_nn, values[:, K : 2 * K], xin[...])
        xall[pl.ds(pl.multiple_of(index * K, K), K), :] = solved

        @pl.when(index < SUB - 1)
        def _():
            following = placed(jnp.minimum(index + 1, SUB - 1))
            xin[...] = following - triple(dot_tn, values[:, 0:K], solved)

        return carry

    @pl.when(head)
    def _():
        arrive(chain, chain_recv_sem, 0)
        pivot = lax.fori_loop(0, 1, factor, chain[0][:, 0:K])
        start_border()
        lax.fori_loop(1, SUB, factor, pivot)

    @pl.when(jnp.logical_not(head))
    def _():
        start_border()

    @pl.when(head)
    def _():
        upper = iota((K, K), 0) <= iota((K, K), 1)
        factor_out[:, 0:K] = jnp.where(upper, pivots[sub, :, 0:K], 0.0).T
        factor_out[:, K : 2 * K] = solver[jnp.maximum(sub - 1, 0), :, 0:K].T
        for step in range(1, SUB):
            line(chain, chain_send_sem, chain_recv_sem, step).wait_send()
        for which in range(2):
            cross(border, border_recv_sem, which).wait_send()
            for index in range(SUB):
                result(index, which).wait_send()

    @pl.when(second | third)
    def _():
        landed(border, border_recv_sem, sub).wait_recv()
        for step in range(1, SUB):
            line(border, border_send_sem, border_recv_sem, step).start()
        for slot in range(SUB):
            arrive(border, border_recv_sem, slot)
        xin[...] = placed(0)
        lax.fori_loop(0, SUB, solve, 0)
        odd = lax.rem(sub, 2) == 1
        mine = xall[:, own_tile]
        turned = mine.T
        factor_out[...] = jnp.where(odd, turned[K:], turned[0:K])
        product = triple(dot_tn, mine, xall[...])
        product_out[...] = jnp.where(odd, product[K:], product[0:K])
        for step in range(1, SUB):
            line(border, border_send_sem, border_recv_sem, step).wait_send()


def place_kernel(own_hbm, factors_hbm, product_hbm, out, own, factors, product, sems):
    copies = [
        pltpu.make_async_copy(source, target, sems.at[n])
        for n, (source, target) in enumerate(
            ((own_hbm, own), (factors_hbm, factors), (product_hbm, product))
        )
    ]
    for copy in copies:
        copy.start()
    mrow = lax.axis_index("mrow")
    mcol = lax.axis_index("mcol")
    sub = lax.axis_index("sub")
    mrows = lax.axis_size("mrow")
    mcols = lax.axis_size("mcol")
    position = (mrow * mcols + mcol) * SUB + sub
    head = (mrow == 0) & (mcol == 0)
    second = (mrow == 0) & (mcol == 1)
    third = (mrow == 1) & (mcol == 0)
    odd = lax.rem(sub, 2) == 1

    out[...] = jnp.zeros_like(out)
    for copy in copies:
        copy.wait()

    def tile(index):
        return pl.ds(pl.multiple_of(index * 128, 128), 128)

    def block(index):
        return own[:, index * K : (index + 1) * K]

    empty = jnp.zeros((K, K), F32)

    @pl.when(jnp.logical_not(head))
    def _():
        diagonal, x_high, y_high, z_high, x_low, y_low, z_low = (block(n) for n in range(7))
        here = position // 2
        pair_even = jnp.concatenate([diagonal, x_high], axis=1)
        pair_odd = jnp.concatenate([x_low, diagonal], axis=1)
        out[:, tile(here)] = jnp.where(odd, pair_odd, pair_even)

        @pl.when(odd & (sub < SUB - 1))
        def _():
            out[:, tile(here + 1)] = jnp.concatenate([x_high, empty], axis=1)

        @pl.when(jnp.logical_not(odd) & (sub > 0))
        def _():
            out[:, tile(here - 1)] = jnp.concatenate([empty, x_low], axis=1)

        def either(value):
            return jnp.where(
                odd,
                jnp.concatenate([empty, value], axis=1),
                jnp.concatenate([value, empty], axis=1),
            )

        for value, present, stride in (
            (y_high, mcol < mcols - 1, SUB // 2),
            (y_low, (mcol > 0) & jnp.logical_not(second), -(SUB // 2)),
            (z_high, mrow < mrows - 1, mcols * SUB // 2),
            (z_low, (mrow > 0) & jnp.logical_not(third), -(mcols * SUB // 2)),
        ):

            @pl.when(present)
            def _():
                out[:, tile(here + stride)] = either(value)

    @pl.when(head)
    def _():
        mine = factors[:, 0:K]
        before = factors[:, K : 2 * K]
        here = sub // 2
        out[:, tile(here)] = jnp.where(
            odd,
            jnp.concatenate([before, mine], axis=1),
            jnp.concatenate([mine, empty], axis=1),
        )

        @pl.when(jnp.logical_not(odd) & (sub > 0))
        def _():
            out[:, tile(here - 1)] = jnp.concatenate([empty, before], axis=1)

    @pl.when(second | third)
    def _():
        out[:, 0 : 8 * K] = factors[...]
        out[:, 8 * K : 16 * K] -= product[:, 0 : 8 * K]
        far = mcols * SUB * K
        out[:, far : far + 8 * K] -= product[:, 8 * K : 16 * K]


def shards(deflation, reaction, vector_counts):
    vmem = pl.BlockSpec(memory_space=pltpu.VMEM)
    results = pl.pallas_call(
        assemble_kernel,
        out_shape=(
            jax.ShapeDtypeStruct((K, 8 * K), F32),
            jax.ShapeDtypeStruct((K, 8 * K), F32),
            jax.ShapeDtypeStruct((K, 16 * K), F32),
        ),
        in_specs=[
            pl.BlockSpec(memory_space=pl.ANY),
            pl.BlockSpec(memory_space=pl.ANY),
            pl.BlockSpec(memory_space=pltpu.SMEM),
        ],
        out_specs=(vmem, vmem, vmem),
        scratch_shapes=[
            pltpu.VMEM((CX + 1, K, CY, CZ), BF16),
            pltpu.VMEM((ROWS + 16, 8 * CZ), BF16),
            pltpu.VMEM((ROWS, 8 * CZ), BF16),
            pltpu.VMEM((ROWS, ROWS), F32),
            pltpu.VMEM((CX, CY, CZ), F32),
            pltpu.VMEM((CX, 16, ROWS), F32),
            pltpu.VMEM((2, K, CZ), F32),
            pltpu.VMEM((CX, K, CZ), BF16),
            pltpu.VMEM((CX, K, CZ), BF16),
            pltpu.VMEM((CX, K, CZ), BF16),
            pltpu.VMEM((CX, 8, ROWS), F32),
            pltpu.VMEM((K, CY // 2, CZ), BF16),
            pltpu.VMEM((K, CY // 2, CZ), BF16),
            pltpu.VMEM((8, 128), F32),
            pltpu.VMEM((6, 8, 128), F32),
            pltpu.VMEM((4, K, 128), F32),
            pltpu.VMEM((4, K, 128), F32),
            pltpu.VMEM((SUB, K, 2 * K), F32),
            pltpu.VMEM((SUB, K, 2 * K), F32),
            pltpu.VMEM((SUB, K, 128), F32),
            pltpu.VMEM((SUB, K, 2 * K), F32),
            pltpu.VMEM((2, 8, 8, 128), F32),
            pltpu.VMEM((K, 16 * K), F32),
            pltpu.VMEM((SUB * K, 16 * K), F32),
            pltpu.SemaphoreType.DMA((CX,)),
            pltpu.SemaphoreType.DMA,
            pltpu.SemaphoreType.DMA((6,)),
            pltpu.SemaphoreType.DMA((6,)),
            pltpu.SemaphoreType.DMA((2,)),
            pltpu.SemaphoreType.DMA((2,)),
            pltpu.SemaphoreType.DMA((CX,)),
            pltpu.SemaphoreType.DMA((CX,)),
            pltpu.SemaphoreType.DMA((CX,)),
            pltpu.SemaphoreType.DMA((CX,)),
            pltpu.SemaphoreType.DMA((4,)),
            pltpu.SemaphoreType.DMA((4,)),
            pltpu.SemaphoreType.DMA((SUB,)),
            pltpu.SemaphoreType.DMA((SUB,)),
            pltpu.SemaphoreType.DMA((SUB,)),
            pltpu.SemaphoreType.DMA((SUB,)),
            pltpu.SemaphoreType.DMA((2,)),
            pltpu.SemaphoreType.DMA((SUB, 2)),
            pltpu.SemaphoreType.DMA((SUB,)),
        ],
        compiler_params=pltpu.CompilerParams(
            collective_id=0, has_side_effects=True, vmem_limit_bytes=56 * 1024 * 1024
        ),
        name="assemble",
    )(deflation, reaction, vector_counts)
    return pl.pallas_call(
        place_kernel,
        out_shape=jax.ShapeDtypeStruct((K, 128 * K), F32),
        in_specs=[pl.BlockSpec(memory_space=pl.ANY)] * 3,
        out_specs=vmem,
        scratch_shapes=[
            pltpu.VMEM((K, 8 * K), F32),
            pltpu.VMEM((K, 8 * K), F32),
            pltpu.VMEM((K, 16 * K), F32),
            pltpu.SemaphoreType.DMA((3,)),
        ],
        compiler_params=pltpu.CompilerParams(vmem_limit_bytes=56 * 1024 * 1024),
        name="place",
    )(*results)


def solution(mesh):
    return jax.shard_map(
        shards,
        mesh=mesh,
        in_specs=(
            P(None, "sub", "mcol", "mrow"),
            P("sub", "mcol", "mrow"),
            P(("mrow", "mcol", "sub")),
        ),
        out_specs=P(("mrow", "mcol", "sub"), None),
        check_vma=False,
    )
```

```python
import functools

import jax
import jax.numpy as jnp
from jax import lax
from jax.experimental import pallas as pl
from jax.experimental.pallas import tpu as pltpu
from jax.sharding import PartitionSpec as P

MESH = pl.DeviceIdType.MESH
F32 = jnp.float32
BF16 = jnp.bfloat16
HI = lax.Precision.HIGHEST
K = 64
CX = 8
CY = 64
CZ = 256
ROWS = K * 8
SUB = 8
EARLY = 6


def dot_nt(a, b, precision=None):
    return lax.dot_general(
        a, b, (((1,), (1,)), ((), ())), precision=precision, preferred_element_type=F32
    )


def dot_nn(a, b, precision=None):
    return lax.dot_general(
        a, b, (((1,), (0,)), ((), ())), precision=precision, preferred_element_type=F32
    )


def dot_tn(a, b, precision=None):
    return lax.dot_general(
        a, b, (((0,), (0,)), ((), ())), precision=precision, preferred_element_type=F32
    )


def halves(value):
    high = value.astype(BF16)
    return high, (value - high.astype(F32)).astype(BF16)


def triple(dot, a, b):
    a_high, a_low = halves(a)
    b_high, b_low = halves(b)
    return dot(a_high, b_high) + (dot(a_high, b_low) + dot(a_low, b_high))


def iota(shape, axis):
    return lax.broadcasted_iota(jnp.int32, shape, axis)


def fold(product):
    same = (iota(product.shape, 0) & 7) == (iota(product.shape, 1) & 7)
    kept = jnp.where(same, product, 0.0).reshape(K, 8, ROWS).sum(axis=1)
    collect = ((iota((ROWS, K), 0) >> 3) == iota((ROWS, K), 1)).astype(F32)
    collect = collect.astype(BF16)
    high, rest = kept.astype(BF16), kept - kept.astype(BF16).astype(F32)
    middle, low = halves(rest)
    return dot_nn(high, collect) + (dot_nn(middle, collect) + dot_nn(low, collect))


def assemble_kernel(
    defl,
    react,
    count,
    own_out,
    factor_out,
    product_out,
    mbuf,
    left,
    right,
    acc,
    weight,
    zrows,
    yedge,
    ylow,
    yhigh,
    yrecv,
    zrecv,
    xrecv_low,
    xrecv_high,
    mask_own,
    mask_recv,
    part_send,
    part_recv,
    chain,
    border,
    pivots,
    solver,
    spread,
    xin,
    xall,
    load_sem,
    field_sem,
    mask_send_sem,
    mask_recv_sem,
    face_send_sem,
    face_recv_sem,
    y_send_sem,
    y_recv_sem,
    z_send_sem,
    z_recv_sem,
    part_send_sem,
    part_recv_sem,
    chain_send_sem,
    chain_recv_sem,
    border_send_sem,
    border_recv_sem,
    cross_send_sem,
    solver_send_sem,
    solver_recv_sem,
):
    mrow = lax.axis_index("mrow")
    mcol = lax.axis_index("mcol")
    sub = lax.axis_index("sub")
    mrows = lax.axis_size("mrow")
    mcols = lax.axis_size("mcol")
    s_next, s_prev = lax.rem(sub + 1, SUB), lax.rem(sub + SUB - 1, SUB)
    j_next, j_prev = lax.rem(mcol + 1, mcols), lax.rem(mcol + mcols - 1, mcols)
    i_next, i_prev = lax.rem(mrow + 1, mrows), lax.rem(mrow + mrows - 1, mrows)
    head = (mrow == 0) & (mcol == 0)
    second = (mrow == 0) & (mcol == 1)
    third = (mrow == 1) & (mcol == 0)

    loads = [
        pltpu.make_async_copy(defl.at[:, x], mbuf.at[x], load_sem.at[x]) for x in range(CX)
    ]
    field = pltpu.make_async_copy(react, weight, field_sem)
    for load in loads[0:2]:
        load.start()
    field.start()
    loads[2].start()

    barrier = pltpu.get_barrier_semaphore()
    for step in range(1, SUB):
        pl.semaphore_signal(
            barrier,
            inc=1,
            device_id={"sub": lax.rem(sub + step, SUB)},
            device_id_type=MESH,
        )
    for axis, other in (
        ("mcol", j_next),
        ("mcol", j_prev),
        ("mrow", i_next),
        ("mrow", i_prev),
    ):
        pl.semaphore_signal(barrier, inc=1, device_id={axis: other}, device_id_type=MESH)

    live = count[0]
    mask_own[...] = (iota((8, 128), 1) < live).astype(F32)
    mbuf[CX] = jnp.zeros((K, CY, CZ), BF16)
    acc[...] = jnp.zeros_like(acc)
    part_send[...] = jnp.zeros_like(part_send)
    tail = iota((16, 8 * CZ), 0)
    spot = (tail & 7) * CZ + (tail >> 3) * (CZ - 1)
    left[ROWS : ROWS + 16, :] = (iota((16, 8 * CZ), 1) == spot).astype(F32).astype(BF16)

    def remote(src, dst, send, recv, target):
        return pltpu.make_async_remote_copy(
            src_ref=src,
            dst_ref=dst,
            send_sem=send,
            recv_sem=recv,
            device_id=target,
            device_id_type=MESH,
        )

    xface_up = remote(
        defl.at[:, CX - 1, 0 : CY // 2],
        xrecv_low,
        face_send_sem.at[0],
        face_recv_sem.at[0],
        {"sub": s_next},
    )
    xface_down = remote(
        defl.at[:, 0, CY // 2 : CY],
        xrecv_high,
        face_send_sem.at[1],
        face_recv_sem.at[1],
        {"sub": s_prev},
    )
    group = 4
    last_lane = iota((1, 1, 128), 2) == 127
    last_row = iota((1, 8, 1), 1) == 7

    def flat(value):
        return value.reshape(8 * group, CZ).astype(BF16)

    def stage_group(x, first, row):
        here = mbuf[x, pl.ds(first, group)].astype(F32)
        after_x = mbuf[x + 1, pl.ds(first, group)].astype(F32)
        turned_low = pltpu.roll(here[:, :, 0:128], 127, 2)
        turned_high = pltpu.roll(here[:, :, 128:256], 127, 2)
        after_z = jnp.concatenate(
            [
                jnp.where(last_lane, turned_high, turned_low),
                jnp.where(last_lane, 0.0, turned_high),
            ],
            axis=2,
        )
        turned = [pltpu.roll(here[:, 8 * n : 8 * n + 8, :], 7, 1) for n in range(8)]
        turned.append(jnp.zeros((group, 8, CZ), F32))
        place = pl.ds(row, 8 * group)
        for block in range(8):
            part = slice(8 * block, 8 * block + 8)
            lanes = slice(block * CZ, (block + 1) * CZ)
            after_y = jnp.where(last_row, turned[block + 1], turned[block])
            half = weight[x, part][None] * here[:, part] - after_x[:, part]
            half = half - after_y - after_z[:, part]
            left[place, lanes] = flat(half)
            right[place, lanes] = flat(here[:, part])
        for n in range(group):
            yedge[0, pl.ds(first + n, 1), :] = here[n, 0:1, :]
            yedge[1, pl.ds(first + n, 1), :] = here[n, CY - 1 : CY, :]

    def y_face(x):
        return remote(
            yhigh.at[x], yrecv.at[x], y_send_sem.at[x], y_recv_sem.at[x], {"mcol": j_next}
        )

    def z_face(x):
        return remote(
            zrows.at[x, pl.ds(8, 8)],
            zrecv.at[x],
            z_send_sem.at[x],
            z_recv_sem.at[x],
            {"mrow": i_next},
        )

    y_up, y_down = mcol < mcols - 1, mcol > 0
    z_up, z_down = mrow < mrows - 1, mrow > 0

    def start_faces(x):
        @pl.when(y_up)
        def _():
            y_face(x).start()

        @pl.when(z_up)
        def _():
            z_face(x).start()

    def silent_plane(x, carry):
        @pl.when(x + 3 < CX)
        def _():
            pltpu.make_async_copy(
                defl.at[:, x + 3], mbuf.at[x + 3], load_sem.at[x + 3]
            ).start()

        @pl.when(x < EARLY)
        def _():
            pltpu.make_async_copy(
                defl.at[:, x + 1], mbuf.at[x + 1], load_sem.at[x + 1]
            ).wait()

        for first in range(0, K, group):
            stage_group(x, first, 8 * first)
        ylow[x] = yedge[0].astype(BF16)
        yhigh[x] = yedge[1].astype(BF16)
        product = dot_nt(left[...], right[...])
        acc[...] += product[:ROWS]
        zrows[x] = product[ROWS : ROWS + 16]
        return carry

    def plane(x, carry):
        silent_plane(x, carry)
        start_faces(x)
        return carry

    field.wait()
    weight[...] = 3.0 + 0.5 * weight[...]
    loads[0].wait()
    lax.fori_loop(0, 1, silent_plane, 0)
    pl.semaphore_wait(barrier, SUB - 1 + 4)
    xface_up.start()
    xface_down.start()

    masks = []
    for slot, target in enumerate(
        (
            {"sub": s_next},
            {"sub": s_prev},
            {"mcol": j_next},
            {"mcol": j_prev},
            {"mrow": i_next},
            {"mrow": i_prev},
        )
    ):
        masks.append(
            remote(
                mask_own,
                mask_recv.at[slot],
                mask_send_sem.at[slot],
                mask_recv_sem.at[slot],
                target,
            )
        )
        masks[-1].start()
    start_faces(0)
    lax.fori_loop(1, EARLY, plane, 0)

    for load in loads[EARLY + 1 :]:
        load.wait()
    xface_up.wait()
    xface_down.wait()

    def stage(step, inner):
        for q in range(2):
            first = pl.multiple_of(8 * step + q * group, group)
            place = pl.ds(pl.multiple_of(64 * step + q * group * 8, group * 8), group * 8)
            chosen = pl.ds(first, group)
            sources = (
                (mbuf[0, chosen, 0 : CY // 2, :], xrecv_low[chosen]),
                (last_half[chosen], xrecv_high[chosen]),
            )
            for which, (mine, theirs) in enumerate(sources):
                mine = mine.astype(F32)
                theirs = theirs.astype(F32)
                for block in range(4):
                    part = slice(8 * block, 8 * block + 8)
                    lanes = slice((4 * which + block) * CZ, (4 * which + block + 1) * CZ)
                    right[place, lanes] = flat(mine[:, part])
                    left[place, lanes] = flat(theirs[:, part])
        return inner

    last_half = mbuf.at[CX - 1, :, CY // 2 : CY, :]
    lax.fori_loop(0, K // 8, stage, 0)
    low_part = fold(dot_nt(left[0:ROWS, 0 : 4 * CZ], right[:, 0 : 4 * CZ]))
    high_part = fold(dot_nt(right[:, 4 * CZ : 8 * CZ], left[0:ROWS, 4 * CZ : 8 * CZ]))
    part_send[0, :, 0:K] = low_part
    part_send[1, :, 0:K] = high_part.T
    parts = [
        remote(
            part_send.at[slot],
            part_recv.at[slot],
            part_send_sem.at[slot],
            part_recv_sem.at[slot],
            target,
        )
        for slot, target in enumerate(
            ({"sub": s_prev}, {"sub": s_next}, {"mcol": j_prev}, {"mrow": i_prev})
        )
    ]
    parts[0].start()
    parts[1].start()

    lax.fori_loop(EARLY, CX, plane, 0)

    own_row = (iota((K, K), 0) < live).astype(F32)
    own_col = mask_own[0:1, 0:K]
    diag = (iota((K, K), 0) == iota((K, K), 1)).astype(F32)

    def finish(block, slot, present):
        kept = own_row * mask_recv[slot, 0:1, 0:K]
        return -block * (kept * jnp.where(present, 1.0, 0.0))

    gram = fold(acc[...])
    diagonal = (gram + gram.T) * own_row * own_col + diag * (1.0 - own_row)
    for mask in masks:
        mask.wait()
    parts[0].wait()
    parts[1].wait()
    x_high = finish(high_part + part_recv[0, :, 0:K], 1, sub < SUB - 1)

    def cross(buffer, recv, which):
        return remote(
            buffer.at[sub],
            buffer.at[sub],
            cross_send_sem.at[which],
            recv.at[sub],
            ({"mcol": j_next}, {"mrow": i_next})[which],
        )

    def line(buffer, send, recv, step):
        return remote(
            buffer.at[sub],
            buffer.at[sub],
            send.at[step],
            recv.at[sub],
            {"sub": lax.rem(sub + step, SUB)},
        )

    def landed(buffer, recv, slot):
        return remote(
            buffer.at[slot],
            buffer.at[slot],
            cross_send_sem.at[0],
            recv.at[slot],
            {"mcol": j_next},
        )

    @pl.when(head)
    def _():
        chain[sub] = jnp.concatenate([diagonal, x_high], axis=1)
        for step in range(1, SUB):
            line(chain, chain_send_sem, chain_recv_sem, step).start()

    x_low = finish(low_part.T + part_recv[1, :, 0:K], 0, sub > 0)
    own_out[:, 0 : 2 * K] = jnp.concatenate([diagonal, x_high], axis=1)
    own_out[:, 4 * K : 5 * K] = x_low

    @pl.when(y_down)
    def _():
        for x in range(CX):
            y_face(x).wait_recv()
        y_part = dot_nt(
            jnp.concatenate([yrecv[x] for x in range(CX)], axis=1),
            jnp.concatenate([ylow[x] for x in range(CX)], axis=1),
        )
        part_send[2, :, 0:K] = y_part
        parts[2].start()
        own_out[:, 5 * K : 6 * K] = finish(y_part.T, 2, True)

    @pl.when(z_down)
    def _():
        for x in range(CX):
            z_face(x).wait_recv()
        z_low = zrows[:, 0:8, :].reshape(K, ROWS)
        z_part = fold(dot_tn(zrecv[...].reshape(K, ROWS), z_low))
        part_send[3, :, 0:K] = z_part
        parts[3].start()
        own_out[:, 6 * K : 7 * K] = finish(z_part.T, 4, True)

    def start_border():
        for up, down, part, face in (
            (y_up, y_down, parts[2], y_face),
            (z_up, z_down, parts[3], z_face),
        ):

            @pl.when(up)
            def _():
                part.wait_recv()
                for x in range(CX):
                    face(x).wait_send()

            @pl.when(down)
            def _():
                part.wait_send()

        y_high = finish(part_recv[2, :, 0:K], 3, y_up)
        z_high = finish(part_recv[3, :, 0:K], 5, z_up)
        own_out[:, 2 * K : 4 * K] = jnp.concatenate([y_high, z_high], axis=1)

        @pl.when(head)
        def _():
            border[sub] = jnp.concatenate([y_high, z_high], axis=1)
            cross(border, border_recv_sem, 0).start()
            cross(border, border_recv_sem, 1).start()

    def eliminate(index, pivot):
        coupling = chain[index][:, K : 2 * K]
        unit = (iota((K, K), 0) == iota((K, K), 1)).astype(F32)
        state = jnp.concatenate([pivot, jnp.zeros((K, K), F32)], axis=1)
        extra = jnp.concatenate([coupling, unit], axis=1)
        state = [state[8 * n : 8 * n + 8] for n in range(8)]
        inverse = [extra[8 * n : 8 * n + 8] for n in range(8)]
        for now in range(8):
            columns = {
                n: [
                    jnp.broadcast_to(state[n][:, 8 * now + c : 8 * now + c + 1], (8, 128))
                    for c in range(8)
                ]
                for n in range(now, 8)
            }
            for c in range(8):
                spread[now % 2, c] = columns[now][c]

            def entry(r, c):
                return jnp.broadcast_to(spread[now % 2, c, r : r + 1, :], (8, 128))

            lower = {}
            scale = []
            for c in range(8):
                value = entry(c, c)
                for k in range(c):
                    value = value - lower[c, k] * lower[c, k]
                scale.append(lax.rsqrt(value))
                for r in range(c + 1, 8):
                    value = entry(r, c)
                    for k in range(c):
                        value = value - lower[r, k] * lower[c, k]
                    lower[r, c] = value * scale[c]
            lines, lines_inverse = [], []
            for c in range(8):
                line_now = state[now][c : c + 1]
                line_inverse = inverse[now][c : c + 1]
                for k in range(c):
                    line_now = line_now - lower[c, k] * lines[k]
                    line_inverse = line_inverse - lower[c, k] * lines_inverse[k]
                lines.append(line_now * scale[c])
                lines_inverse.append(line_inverse * scale[c])
                at = 8 * now + c
                pivots[index, at : at + 1, :] = lines[c][0:1]
                solver[index, at : at + 1, :] = lines_inverse[c][0:1]
            for n in range(now + 1, 8):
                factors = []
                for c in range(8):
                    factor = columns[n][c]
                    for k in range(c):
                        factor = factor - factors[k] * lower[c, k]
                    factors.append(factor * scale[c])
                for c in range(8):
                    state[n] = state[n] - factors[c] * lines[c]
                    inverse[n] = inverse[n] - factors[c] * lines_inverse[c]

    def arrive(buffer, recv, slot):
        @pl.when(sub != slot)
        def _():
            landed(buffer, recv, slot).wait_recv()

    def result(index, which):
        return remote(
            solver.at[index],
            solver.at[index],
            solver_send_sem.at[index, which],
            solver_recv_sem.at[index],
            ({"mcol": j_next}, {"mrow": i_next})[which],
        )

    def factor(index, pivot):
        following = jnp.minimum(index + 1, SUB - 1)

        @pl.when(index < SUB - 1)
        def _():
            arrive(chain, chain_recv_sem, following)

        eliminate(index, pivot)
        result(index, 0).start()
        result(index, 1).start()
        coupled = solver[index, :, 0:K]
        return chain[following][:, 0:K] - dot_tn(coupled, coupled, HI)

    lane = iota((K, 8 * K), 1) >> 6

    def placed(index):
        values = border[index]
        first = jnp.concatenate([values[:, 0:K]] * 8, axis=1)
        other = jnp.concatenate([values[:, K : 2 * K]] * 8, axis=1)
        first = jnp.where(lane == index, first, 0.0)
        other = jnp.where(lane == index, other, 0.0)
        return jnp.concatenate([first, other], axis=1)

    own_slot = jnp.where(third, SUB, 0) + sub
    own_tile = pl.ds(pl.multiple_of((own_slot // 2) * 128, 128), 128)

    def solve(index, carry):
        result(index, 0).wait_recv()
        values = solver[index]
        solved = triple(dot_nn, values[:, K : 2 * K], xin[...])
        xall[pl.ds(pl.multiple_of(index * K, K), K), :] = solved

        @pl.when(index < SUB - 1)
        def _():
            following = placed(jnp.minimum(index + 1, SUB - 1))
            xin[...] = following - triple(dot_tn, values[:, 0:K], solved)

        return carry

    @pl.when(head)
    def _():
        arrive(chain, chain_recv_sem, 0)
        pivot = lax.fori_loop(0, 1, factor, chain[0][:, 0:K])
        start_border()
        lax.fori_loop(1, SUB, factor, pivot)

    @pl.when(jnp.logical_not(head))
    def _():
        start_border()

    @pl.when(head)
    def _():
        upper = iota((K, K), 0) <= iota((K, K), 1)
        factor_out[:, 0:K] = jnp.where(upper, pivots[sub, :, 0:K], 0.0).T
        factor_out[:, K : 2 * K] = solver[jnp.maximum(sub - 1, 0), :, 0:K].T
        for step in range(1, SUB):
            line(chain, chain_send_sem, chain_recv_sem, step).wait_send()
        for which in range(2):
            cross(border, border_recv_sem, which).wait_send()
            for index in range(SUB):
                result(index, which).wait_send()

    @pl.when(second | third)
    def _():
        landed(border, border_recv_sem, sub).wait_recv()
        for step in range(1, SUB):
            line(border, border_send_sem, border_recv_sem, step).start()
        for slot in range(SUB):
            arrive(border, border_recv_sem, slot)
        xin[...] = placed(0)
        lax.fori_loop(0, SUB, solve, 0)
        odd = lax.rem(sub, 2) == 1
        mine = xall[:, own_tile]
        turned = mine.T
        factor_out[...] = jnp.where(odd, turned[K:], turned[0:K])
        product = triple(dot_tn, mine, xall[...])
        product_out[...] = jnp.where(odd, product[K:], product[0:K])
        for step in range(1, SUB):
            line(border, border_send_sem, border_recv_sem, step).wait_send()


def place_kernel(own_hbm, factors_hbm, product_hbm, out, own, factors, product, sems):
    copies = [
        pltpu.make_async_copy(source, target, sems.at[n])
        for n, (source, target) in enumerate(
            ((own_hbm, own), (factors_hbm, factors), (product_hbm, product))
        )
    ]
    for copy in copies:
        copy.start()
    mrow = lax.axis_index("mrow")
    mcol = lax.axis_index("mcol")
    sub = lax.axis_index("sub")
    mrows = lax.axis_size("mrow")
    mcols = lax.axis_size("mcol")
    position = (mrow * mcols + mcol) * SUB + sub
    head = (mrow == 0) & (mcol == 0)
    second = (mrow == 0) & (mcol == 1)
    third = (mrow == 1) & (mcol == 0)
    odd = lax.rem(sub, 2) == 1

    out[...] = jnp.zeros_like(out)
    for copy in copies:
        copy.wait()

    def tile(index):
        return pl.ds(pl.multiple_of(index * 128, 128), 128)

    def block(index):
        return own[:, index * K : (index + 1) * K]

    empty = jnp.zeros((K, K), F32)

    @pl.when(jnp.logical_not(head))
    def _():
        diagonal, x_high, y_high, z_high, x_low, y_low, z_low = (block(n) for n in range(7))
        here = position // 2
        pair_even = jnp.concatenate([diagonal, x_high], axis=1)
        pair_odd = jnp.concatenate([x_low, diagonal], axis=1)
        out[:, tile(here)] = jnp.where(odd, pair_odd, pair_even)

        @pl.when(odd & (sub < SUB - 1))
        def _():
            out[:, tile(here + 1)] = jnp.concatenate([x_high, empty], axis=1)

        @pl.when(jnp.logical_not(odd) & (sub > 0))
        def _():
            out[:, tile(here - 1)] = jnp.concatenate([empty, x_low], axis=1)

        def either(value):
            return jnp.where(
                odd,
                jnp.concatenate([empty, value], axis=1),
                jnp.concatenate([value, empty], axis=1),
            )

        for value, present, stride in (
            (y_high, mcol < mcols - 1, SUB // 2),
            (y_low, (mcol > 0) & jnp.logical_not(second), -(SUB // 2)),
            (z_high, mrow < mrows - 1, mcols * SUB // 2),
            (z_low, (mrow > 0) & jnp.logical_not(third), -(mcols * SUB // 2)),
        ):

            @pl.when(present)
            def _():
                out[:, tile(here + stride)] = either(value)

    @pl.when(head)
    def _():
        mine = factors[:, 0:K]
        before = factors[:, K : 2 * K]
        here = sub // 2
        out[:, tile(here)] = jnp.where(
            odd,
            jnp.concatenate([before, mine], axis=1),
            jnp.concatenate([mine, empty], axis=1),
        )

        @pl.when(jnp.logical_not(odd) & (sub > 0))
        def _():
            out[:, tile(here - 1)] = jnp.concatenate([empty, before], axis=1)

    @pl.when(second | third)
    def _():
        out[:, 0 : 8 * K] = factors[...]
        out[:, 8 * K : 16 * K] -= product[:, 0 : 8 * K]
        far = mcols * SUB * K
        out[:, far : far + 8 * K] -= product[:, 8 * K : 16 * K]


def shards(deflation, reaction, vector_counts):
    vmem = pl.BlockSpec(memory_space=pltpu.VMEM)
    results = pl.pallas_call(
        assemble_kernel,
        out_shape=(
            jax.ShapeDtypeStruct((K, 8 * K), F32),
            jax.ShapeDtypeStruct((K, 8 * K), F32),
            jax.ShapeDtypeStruct((K, 16 * K), F32),
        ),
        in_specs=[
            pl.BlockSpec(memory_space=pl.ANY),
            pl.BlockSpec(memory_space=pl.ANY),
            pl.BlockSpec(memory_space=pltpu.SMEM),
        ],
        out_specs=(vmem, vmem, vmem),
        scratch_shapes=[
            pltpu.VMEM((CX + 1, K, CY, CZ), BF16),
            pltpu.VMEM((ROWS + 16, 8 * CZ), BF16),
            pltpu.VMEM((ROWS, 8 * CZ), BF16),
            pltpu.VMEM((ROWS, ROWS), F32),
            pltpu.VMEM((CX, CY, CZ), F32),
            pltpu.VMEM((CX, 16, ROWS), F32),
            pltpu.VMEM((2, K, CZ), F32),
            pltpu.VMEM((CX, K, CZ), BF16),
            pltpu.VMEM((CX, K, CZ), BF16),
            pltpu.VMEM((CX, K, CZ), BF16),
            pltpu.VMEM((CX, 8, ROWS), F32),
            pltpu.VMEM((K, CY // 2, CZ), BF16),
            pltpu.VMEM((K, CY // 2, CZ), BF16),
            pltpu.VMEM((8, 128), F32),
            pltpu.VMEM((6, 8, 128), F32),
            pltpu.VMEM((4, K, 128), F32),
            pltpu.VMEM((4, K, 128), F32),
            pltpu.VMEM((SUB, K, 2 * K), F32),
            pltpu.VMEM((SUB, K, 2 * K), F32),
            pltpu.VMEM((SUB, K, 128), F32),
            pltpu.VMEM((SUB, K, 2 * K), F32),
            pltpu.VMEM((2, 8, 8, 128), F32),
            pltpu.VMEM((K, 16 * K), F32),
            pltpu.VMEM((SUB * K, 16 * K), F32),
            pltpu.SemaphoreType.DMA((CX,)),
            pltpu.SemaphoreType.DMA,
            pltpu.SemaphoreType.DMA((6,)),
            pltpu.SemaphoreType.DMA((6,)),
            pltpu.SemaphoreType.DMA((2,)),
            pltpu.SemaphoreType.DMA((2,)),
            pltpu.SemaphoreType.DMA((CX,)),
            pltpu.SemaphoreType.DMA((CX,)),
            pltpu.SemaphoreType.DMA((CX,)),
            pltpu.SemaphoreType.DMA((CX,)),
            pltpu.SemaphoreType.DMA((4,)),
            pltpu.SemaphoreType.DMA((4,)),
            pltpu.SemaphoreType.DMA((SUB,)),
            pltpu.SemaphoreType.DMA((SUB,)),
            pltpu.SemaphoreType.DMA((SUB,)),
            pltpu.SemaphoreType.DMA((SUB,)),
            pltpu.SemaphoreType.DMA((2,)),
            pltpu.SemaphoreType.DMA((SUB, 2)),
            pltpu.SemaphoreType.DMA((SUB,)),
        ],
        compiler_params=pltpu.CompilerParams(
            collective_id=0, has_side_effects=True, vmem_limit_bytes=56 * 1024 * 1024
        ),
        name="assemble",
    )(deflation, reaction, vector_counts)
    return pl.pallas_call(
        place_kernel,
        out_shape=jax.ShapeDtypeStruct((K, 128 * K), F32),
        in_specs=[pl.BlockSpec(memory_space=pl.ANY)] * 3,
        out_specs=vmem,
        scratch_shapes=[
            pltpu.VMEM((K, 8 * K), F32),
            pltpu.VMEM((K, 8 * K), F32),
            pltpu.VMEM((K, 16 * K), F32),
            pltpu.SemaphoreType.DMA((3,)),
        ],
        compiler_params=pltpu.CompilerParams(vmem_limit_bytes=56 * 1024 * 1024),
        name="place",
    )(*results)


def solution(mesh):
    return jax.shard_map(
        shards,
        mesh=mesh,
        in_specs=(
            P(None, "sub", "mcol", "mrow"),
            P("sub", "mcol", "mrow"),
            P(("mrow", "mcol", "sub")),
        ),
        out_specs=P(("mrow", "mcol", "sub"), None),
        check_vma=False,
    )
```
